512 devices in a mesh: domain: 8 (over x, core), fsdp: 64 (over y, z).
Axes of the slice: x: 4, y: 4, z: 16, core: 2. Of those that a mesh axis runs over, the one named last changes fastest.
Arguments:
- gradients: bfloat16 [8, 64, 4096, 512], P('domain', None, 'fsdp')
- row_counts: int32 [64], replicated, may hold values from 2048 to 4096, as said below
- domain_ids: int32 [8], replicated, may hold values from 0 to 7
- domain_weights: float32 [8], replicated, may hold values from 0.2 to 2
Outputs:
- updates: float32 [64, 4096, 512], P('domain', 'fsdp')
- new_weights: float32 [8], replicated
The draws below stay inside these ranges and needn't reach their ends.
Inputs may be any that keep to these rules, and one draw needn't show every extreme that they name: `row_counts`: each matrix has 4096 or 2048 rows, and both counts occur.
All inputs are finite; a program needn't handle non-finite values.
Results may differ from the reference program's by a relative error of at most 0.0071.
Values may be sent and summed in bfloat16 or wider, within the bound.
A program may use at most 64 MiB of HBM per device.

```python
import math
import jax
import jax.numpy as jnp
from jax import lax

ROWS = 4096
LAT = 512
DOMAINS = 8
NS_ITERS = 3
GROUPS = 8
MATS = 64


def draw_gradients(key, part):
    key_rows, key_cols, key_groups, key_base = jax.random.split(key, 4)
    row_axis = jnp.arange(ROWS, dtype=jnp.float32)
    row_scale = jnp.power(10.0, row_axis / ROWS) * jnp.exp(jax.random.uniform(key_rows, (ROWS,), jnp.float32, -0.3, 0.3))
    group_scale = jnp.power(2.0, jax.random.uniform(key_groups, (GROUPS,), jnp.float32, -1.0, 1.0))
    col_scale = jnp.power(10.0, jax.random.uniform(key_cols, (LAT,), jnp.float32, 0.0, 1.0))
    base_part = jax.random.normal(key_base, (GROUPS, MATS, ROWS, LAT), jnp.float32)
    values = base_part * group_scale[:, None, None, None] * row_scale[None, None, :, None] * col_scale[None, None, None, :] * 0.1
    return values.astype(jnp.bfloat16)


def draw_row_counts(key, part):
    key_base, key_first, key_second = jax.random.split(key, 3)
    counts = ROWS - ROWS // 2 * jax.random.randint(key_base, (MATS,), 0, 2)
    first_pos = jax.random.randint(key_first, (), 0, MATS)
    second = (first_pos + 1 + jax.random.randint(key_second, (), 0, MATS - 1)) % MATS
    matrix_pos = jnp.arange(MATS, dtype=jnp.int32)
    counts = jnp.where(matrix_pos == first_pos, ROWS, counts)
    counts = jnp.where(matrix_pos == second, ROWS // 2, counts)
    return counts.astype(jnp.int32)


def with_ends(array, key, least, largest):
    longest = array.shape.index(max(array.shape))
    spots = []
    for shift in (0, 1):
        where = [jax.random.randint(jax.random.fold_in(key, axis), (), 0, length) for axis, length in enumerate(array.shape)]
        where[longest] = (where[longest] + shift) % array.shape[longest]
        spots.append(tuple(where))
    return array.at[spots[0]].set(least).at[spots[1]].set(largest)


def setup_inputs(seed: int = 0) -> dict:
    arg_keys = jax.random.split(jax.random.key(seed), 5)
    gradients = draw_gradients(jax.random.fold_in(arg_keys[4], 71), 0)
    row_counts = draw_row_counts(jax.random.fold_in(arg_keys[4], 71), 0)
    domain_ids = with_ends(jax.random.randint(arg_keys[2], (GROUPS,), 0, DOMAINS), jax.random.fold_in(arg_keys[2], 1), 0, DOMAINS - 1).astype(jnp.int32)
    domain_weights = jnp.clip(jnp.exp(jax.random.uniform(arg_keys[3], (DOMAINS,), jnp.float32, math.log(0.2), math.log(2.0))), 0.2, 2.0)
    return {"gradients": gradients, "row_counts": row_counts, "domain_ids": domain_ids, "domain_weights": domain_weights}


COEF_A = 3.4445
COEF_B = -4.775
COEF_C = 2.0315
MUON_SCALE = 0.2
ETA = 4.0

def group_mixing(domain_ids, domain_weights, kind_count):
    weight_share = domain_weights / jnp.sum(domain_weights)
    onehot = (domain_ids[:, None] == jnp.arange(kind_count, dtype=jnp.int32)[None, :]).astype(jnp.float32)
    counts = lax.optimization_barrier(jnp.sum(onehot, axis=0))
    per_member = weight_share / jnp.maximum(counts, 1.0)
    group_mix = lax.optimization_barrier(jnp.sum(onehot * per_member[None, :], axis=1))
    return (weight_share, onehot, counts, group_mix)

def newton_steps(iterate):
    for repeat in range(NS_ITERS):
        gram_full = lax.dot_general(iterate, iterate, (((0,), (0,)), ((), ())), preferred_element_type=jnp.float32)
        gram_full = lax.optimization_barrier(gram_full.astype(jnp.bfloat16))
        square = jnp.dot(gram_full, gram_full, preferred_element_type=jnp.float32)
        poly_term = (COEF_B * gram_full.astype(jnp.float32) + COEF_C * square).astype(jnp.bfloat16)
        iterate = lax.optimization_barrier((COEF_A * iterate.astype(jnp.float32) + jnp.dot(iterate, poly_term, preferred_element_type=jnp.float32)).astype(jnp.bfloat16))
    return iterate

def reference(gradients, row_counts, domain_ids, domain_weights):
    weight_share, onehot, counts, group_mix = group_mixing(domain_ids, domain_weights, DOMAINS)
    row_index = jnp.arange(ROWS, dtype=jnp.int32)
    update_scale = MUON_SCALE * math.sqrt(ROWS)

    def per_matrix(matrix_pos):
        grads_one = lax.dynamic_index_in_dim(gradients, matrix_pos, 1, keepdims=False)
        row_limit = lax.dynamic_index_in_dim(row_counts, matrix_pos, 0, keepdims=False)
        row_mask = (row_index < row_limit)[None, :, None]
        masked = jnp.where(row_mask, grads_one.astype(jnp.float32), jnp.zeros((), jnp.float32))
        combined = lax.optimization_barrier(jnp.sum(group_mix[:, None, None] * masked, axis=0))
        aligned = lax.optimization_barrier(jnp.sum(masked * combined[None], axis=(1, 2)))
        squares = lax.optimization_barrier(jnp.sum(masked * masked, axis=(1, 2)))
        frob_sq = jnp.sum(combined * combined)
        start = lax.optimization_barrier((combined / (jnp.sqrt(frob_sq) + 1e-07)).astype(jnp.bfloat16))
        finished = newton_steps(start)
        return (finished.astype(jnp.float32) * update_scale, aligned, squares, frob_sq)
    updates, aligned, squares, frob_sq = lax.map(per_matrix, jnp.arange(MATS, dtype=jnp.int32))
    total_sq = jnp.sum(frob_sq)
    cosine = lax.optimization_barrier(jnp.sum(aligned, axis=0)) / (jnp.sqrt(lax.optimization_barrier(jnp.sum(squares, axis=0))) * jnp.sqrt(total_sq) + 1e-06)
    score = lax.optimization_barrier(jnp.sum(onehot * cosine[:, None], axis=0)) / jnp.maximum(counts, 1.0)
    raised = weight_share * jnp.exp(ETA * score)
    return (updates, raised / jnp.sum(raised))
```

```python
import functools
import math

import jax
import jax.numpy as jnp
from jax import lax
from jax.experimental import pallas as pl
from jax.experimental.pallas import tpu as pltpu
from jax.sharding import PartitionSpec as P

COEF_A = 3.4445
COEF_B = -4.775
COEF_C = 2.0315
MUON_SCALE = 0.2
ETA = 4.0
F32 = jnp.float32
BF16 = jnp.bfloat16
CORES = 2
RING = 4


def owner_position(slot, core, y_size, z_size):
    if y_size * z_size != 64:
        return (slot + core) % (y_size * z_size)
    quad, half = slot % 4, slot // 4
    z_pos = 4 * quad + 2 * half + core
    y_pos = (quad + ((0, 2), (1, 0))[half][core]) % 4
    return y_pos * z_size + z_pos


def kernel(
    sizes,
    counts_ref, ids_ref, weights_ref, grads_ref,
    out_ref, new_ref,
    own, sib, far_out, near_out, far_in, near_in, comb, rows, done,
    gram, term, lin0, lin1, gram_b, term_b, lin0_b, lin1_b, score, sq_acc,
    own_sem, sib_send, sib_recv, far_send, far_recv, near_send, near_recv,
    ag_send, ag_recv, agf_send, agf_recv, in_send, in_recv, out_send, out_recv,
    red_send, red_recv,
):
    groups, y_size, z_size, mats, height, width = sizes
    shards = y_size * z_size
    pair = mats // 4
    d = lax.axis_index("domain")
    f = lax.axis_index("fsdp")
    x, core = d // CORES, d % CORES
    y, z = f // z_size, f % z_size
    sibling = CORES * x + (1 - core)
    ring = [(x + step) % RING for step in (2, 1, 3, 0)]
    plus, minus = CORES * ring[1] + core, CORES * ring[2] + core
    owners = [
        jnp.where(
            core == 0,
            owner_position(j, 0, y_size, z_size),
            owner_position(j, 1, y_size, z_size),
        )
        for j in range(mats)
    ]
    own_slot = jnp.int32(0)
    owned = jnp.int32(0)
    for j in range(mats):
        own_slot = jnp.where(f == owners[j], j, own_slot)
        owned = jnp.where(f == owners[j], 1, owned)
    is_owner = owned == 1

    def remote(src, dst, send, recv, dd, ff):
        return pltpu.make_async_remote_copy(
            src_ref=src, dst_ref=dst, send_sem=send, recv_sem=recv,
            device_id=(dd, ff), device_id_type=pl.DeviceIdType.MESH,
        )

    def block(ref, first, count=1):
        return ref.at[pl.ds(first * height, count * height)]

    barrier = pltpu.get_barrier_semaphore()

    def greet(dd, ff):
        pl.semaphore_signal(
            barrier, inc=1, device_id=(dd, ff), device_id_type=pl.DeviceIdType.MESH
        )

    half = mats // 2

    def own_copy(rel, stage):
        first = mats * (CORES * ring[rel] + core) + half * stage
        return pltpu.make_async_copy(
            block(grads_ref, first, half),
            block(own, rel * mats + half * stage, half),
            own_sem.at[rel, stage],
        )

    def sib_copy(rel, stage):
        first = mats * (CORES * ring[rel] + (1 - core)) + half * stage
        return remote(
            block(grads_ref, first, half),
            block(sib, rel * mats + half * stage, half),
            sib_send.at[rel, stage], sib_recv.at[rel, stage], sibling, f,
        )

    order = [(0, 0), (1, 0), (2, 0), (0, 1), (3, 0), (1, 1), (2, 1), (3, 1)]
    for rel, stage in order:
        own_copy(rel, stage).start()

    for step in range(1, groups):
        greet((d + step) % groups, f)
    for step in range(1, y_size):
        greet(d, (y + step) % y_size * z_size + z)
    for step in range(1, z_size):
        greet(d, y * z_size + (z + step) % z_size)
    for j in range(mats):

        @pl.when(f != owners[j])
        def _():
            greet(d, owners[j])

    @pl.when(is_owner)
    def _():
        def one(step, carry):
            greet(d, (f + step) % shards)
            return carry

        lax.fori_loop(1, shards, one, 0)

    pl.semaphore_wait(
        barrier,
        (groups - 1) + (y_size - 1) + (z_size - 1) + mats - owned + owned * (shards - 1),
    )

    for rel, stage in order:
        sib_copy(rel, stage).start()

    total_weight = weights_ref[0]
    for k in range(1, groups):
        total_weight = total_weight + weights_ref[k]

    def mix_row(group):
        kind = ids_ref[group]
        count = jnp.float32(0)
        for h in range(groups):
            count = count + jnp.where(ids_ref[h] == kind, 1.0, 0.0)
        full = lambda value: jnp.full((1, width), value, F32)
        return full(weights_ref[kind]) / full(total_weight) / jnp.maximum(full(count), 1.0)

    mix_own, mix_sib = mix_row(d), mix_row(sibling)

    def keep(rel, j):
        index = mats * (CORES * ring[rel] + core) + j
        return jnp.where(f * height < counts_ref[index], 1.0, 0.0)

    def partial(rel, j):
        at = pl.ds((rel * mats + j) * height, height)
        kept = keep(rel, j)
        return (mix_own * kept) * own[at, :].astype(F32) + (mix_sib * kept) * sib[
            at, :
        ].astype(F32)

    def arrived(rel, stage):
        own_copy(rel, stage).wait()
        sib_copy(rel, stage).wait_recv()

    def far_copy(way, stage):
        part = way * 2 + stage
        return remote(
            block(far_out, part * pair, pair), block(far_in, part * pair, pair),
            far_send.at[part], far_recv.at[part], (plus, minus)[way], f,
        )

    def near_copy(way, quarter):
        first = way * mats + quarter * pair
        return remote(
            block(near_out, first, pair), block(near_in, first, pair),
            near_send.at[way, quarter], near_recv.at[way, quarter], (plus, minus)[way], f,
        )

    def send_far(stage):
        arrived(0, stage)
        for way in (0, 1):
            for i in range(pair):
                at = pl.ds(((way * 2 + stage) * pair + i) * height, height)
                far_out[at, :] = partial(0, (2 * stage + way) * pair + i).astype(BF16)
            far_copy(way, stage).start()

    def send_near(stage):
        for way in (0, 1):
            arrived(1 + way, stage)
            quarter = 2 * stage + 1 - way
            for i in range(pair):
                j = quarter * pair + i
                at = pl.ds((way * mats + j) * height, height)
                near_out[at, :] = partial(1 + way, j).astype(BF16)
            near_copy(way, quarter).start()

    def send_merged(stage):
        for way in (0, 1):
            far_copy(way, stage).wait_recv()
            quarter = 2 * stage + way
            for i in range(pair):
                j = quarter * pair + i
                at = pl.ds((way * mats + j) * height, height)
                came = pl.ds(((way * 2 + stage) * pair + i) * height, height)
                near_out[at, :] = (
                    partial(1 + way, j) + far_in[came, :].astype(F32)
                ).astype(BF16)
            near_copy(way, quarter).start()

    slot_here = z * y_size + y

    def in_copy(j):
        return remote(
            block(comb, 3 * mats + j), block(rows, slot_here),
            in_send.at[j], in_recv.at[z], d, owners[j],
        )

    def combine(stage):
        arrived(3, stage)
        for quarter in (2 * stage, 2 * stage + 1):
            for way in (0, 1):
                near_copy(way, quarter).wait_recv()
            for i in range(pair):
                j = quarter * pair + i
                left = pl.ds(j * height, height)
                right = pl.ds((mats + j) * height, height)
                value = partial(3, j) + (
                    near_in[left, :].astype(F32) + near_in[right, :].astype(F32)
                )
                sq_acc[...] += jnp.sum(
                    (value * value).reshape(height // 8, 8, width), axis=0
                )
                comb[pl.ds((3 * mats + j) * height, height), :] = value.astype(BF16)

                @pl.when(f != owners[j])
                def _():
                    in_copy(j).start()

                @pl.when(f == owners[j])
                def _():
                    pltpu.make_async_copy(
                        block(comb, 3 * mats + j), block(rows, slot_here), in_recv.at[z]
                    ).start()

    sq_acc[...] = jnp.zeros_like(sq_acc)
    send_far(0)
    send_near(0)
    send_far(1)
    send_merged(0)
    send_near(1)
    combine(0)
    send_merged(1)
    combine(1)

    def ag_copy(way, quarter):
        first = quarter * pair
        return remote(
            block(comb, 3 * mats + first, pair),
            block(comb, (2, 1)[way] * mats + first, pair),
            ag_send.at[way, quarter], ag_recv.at[way, quarter], (plus, minus)[way], f,
        )

    def agf_copy(way, stage):
        first = (2 * stage + way) * pair
        return remote(
            block(comb, (2, 1)[way] * mats + first, pair), block(comb, first, pair),
            agf_send.at[way, stage], agf_recv.at[way, stage], (plus, minus)[way], f,
        )

    for quarter in range(4):
        for way in (0, 1):
            ag_copy(way, quarter).start()

    band = y_size * height

    def near_z(step):
        shift = jnp.where(step % 2 == 1, (step + 1) // 2, z_size - step // 2)
        return (z + shift) % z_size

    @pl.when(is_owner)
    def _():
        gram[...] = jnp.zeros_like(gram)

        def one(step, carry):
            zz = near_z(step)
            here = rows.at[pl.ds(zz * band, band)]
            pltpu.make_async_copy(here, here, in_recv.at[zz]).wait()
            part = here[...]
            gram[...] += lax.dot_general(
                part, part, (((0,), (0,)), ((), ())), preferred_element_type=F32
            )
            return carry

        lax.fori_loop(0, z_size, one, 0)

    for stage in (0, 1):
        for way in (0, 1):
            ag_copy(way, 2 * stage + way).wait_recv()
            agf_copy(way, stage).start()

    def out_copy(y_to, z_to):
        slot = z_to * y_size + y_to
        return remote(
            block(done, slot), block(out_ref, own_slot),
            out_send.at[slot], out_recv.at[own_slot], d, y_to * z_size + z_to,
        )

    @pl.when(is_owner)
    def _():
        row_id = lax.broadcasted_iota(jnp.int32, (width, width), 0)
        col_id = lax.broadcasted_iota(jnp.int32, (width, width), 1)
        trace = jnp.sum(jnp.where(row_id == col_id, gram[...], 0.0), axis=0, keepdims=True)
        trace = jnp.sum(trace, axis=1, keepdims=True)
        scale = 1.0 / (jnp.sqrt(trace) + 1e-07)
        dot = lambda a, b: jnp.dot(a[...], b[...], preferred_element_type=F32)

        gram[...] = gram[...] * scale * scale
        gram_b[...] = gram[...].astype(BF16)
        for lin, lin_b in ((lin0, lin0_b), (lin1, lin1_b)):
            lin[...] = COEF_B * gram[...] + COEF_C * dot(gram_b, gram_b)
            lin_b[...] = lin[...].astype(BF16)
            term[...] = COEF_A * gram[...] + dot(lin_b, gram_b)
            term_b[...] = term[...].astype(BF16)
            gram[...] = COEF_A * term[...] + dot(lin_b, term_b)
            gram_b[...] = gram[...].astype(BF16)
        lin0[...] = COEF_A * (lin0[...] + lin1[...]) + dot(lin0_b, lin1_b)
        lin0_b[...] = lin0[...].astype(BF16)
        lin1[...] = COEF_B * gram[...] + COEF_C * dot(gram_b, gram_b)
        lin1_b[...] = lin1[...].astype(BF16)
        whole = COEF_A**2 * lin1[...] + COEF_A * lin0[...] + dot(lin0_b, lin1_b)
        whole = whole + jnp.where(row_id == col_id, COEF_A**3, 0.0)
        gram_b[...] = (whole * scale).astype(BF16)

        def one(step, carry):
            zz = near_z(z_size - 1 - step)
            at = pl.ds(zz * band, band)
            done[at, :] = jnp.dot(
                rows[at, :], gram_b[...], preferred_element_type=F32
            ).astype(BF16)
            for y_to in range(y_size):
                here = y_to * z_size + zz == f

                @pl.when(jnp.logical_not(here))
                def _():
                    out_copy(y_to, zz).start()

                @pl.when(here)
                def _():
                    pltpu.make_async_copy(
                        block(done, slot_here), block(out_ref, own_slot),
                        out_recv.at[own_slot],
                    ).start()

            return carry

        lax.fori_loop(0, z_size, one, 0)

    for way in (0, 1):
        for quarter in range(4):
            if quarter % 2 != way:
                ag_copy(way, quarter).wait_recv()
        for stage in (0, 1):
            agf_copy(way, stage).wait_recv()

    fold = lambda value: jnp.sum(value.reshape(height // 8, 8, width), axis=0)

    def align(index, carry):
        rel, j = index // mats, index % mats
        step = jnp.where(rel == 0, 2, jnp.where(rel == 1, 1, jnp.where(rel == 2, 3, 0)))
        matrix = mats * (CORES * ((x + step) % RING) + core) + j
        kept = jnp.where(f * height < counts_ref[matrix], 1.0, 0.0)
        at = pl.ds(index * height, height)
        mine, other = own[at, :].astype(F32), sib[at, :].astype(F32)
        both = comb[at, :].astype(F32)
        return (
            carry[0] + fold(mine * both),
            carry[1] + fold(other * both),
            carry[2] + kept * fold(mine * mine),
            carry[3] + kept * fold(other * other),
        )

    empty = jnp.zeros((8, width), F32)
    sums = lax.fori_loop(0, RING * mats, align, (empty,) * 4)
    sums = [
        jnp.sum(jnp.sum(value, axis=0, keepdims=True), axis=1, keepdims=True)
        for value in (*sums, sq_acc[...])
    ]
    sub = lax.broadcasted_iota(jnp.int32, (8, 128), 0)
    lane = lax.broadcasted_iota(jnp.int32, (8, 128), 1)

    def by_group(mine, other):
        return jnp.where(sub == d, mine, jnp.where(sub == sibling, other, 0.0))

    tile = jnp.where(
        lane == 0,
        by_group(sums[0], sums[1]),
        jnp.where(
            lane == 1,
            by_group(sums[2], sums[3]),
            jnp.where(lane == 2, sums[4], 0.0),
        ),
    )
    base = 0
    for size, place, where in (
        (groups, d, lambda to: (to, f)),
        (y_size, y, lambda to: (d, to * z_size + z)),
        (z_size, z, lambda to: (d, y * z_size + to)),
    ):
        score[base + place] = tile

        def red_copy(step, base=base, size=size, place=place, where=where):
            return remote(
                score.at[base + place], score.at[base + place],
                red_send.at[base + step], red_recv.at[base + place],
                *where((place + step) % size),
            )

        def red_wait(step, base=base, size=size, place=place):
            came = score.at[base + (place + step) % size]
            pltpu.make_async_copy(
                came, came, red_recv.at[base + (place + step) % size]
            ).wait()

        for step in range(1, size):
            red_copy(step).start()
        for step in range(1, size):
            red_wait(step)
        tile = score[base]
        for i in range(1, size):
            tile = tile + score[base + i]
        for step in range(1, size):
            red_copy(step).wait_send()
        base += size

    id_col = jnp.zeros((8, 128), jnp.int32)
    weight_row = jnp.zeros((1, 128), F32)
    for g in range(groups):
        id_col = jnp.where(sub == g, ids_ref[g], id_col)
        weight_row = jnp.where(lane[:1] == g, weights_ref[g], weight_row)
    column = lambda k: jnp.sum(jnp.where(lane == k, tile, 0.0), axis=1, keepdims=True)
    aligned, squares, total_sq = column(0), column(1), column(2)
    cosine = aligned / (jnp.sqrt(squares) * jnp.sqrt(total_sq) + 1e-06)
    onehot = jnp.where(id_col == lane, 1.0, 0.0)
    kind_counts = jnp.sum(onehot, axis=0, keepdims=True)
    points = jnp.sum(onehot * cosine, axis=0, keepdims=True) / jnp.maximum(kind_counts, 1.0)
    share = weight_row / jnp.full((1, 128), total_weight, F32)
    raised = share * jnp.exp(ETA * points)
    new_ref[...] = raised / jnp.sum(raised, axis=1, keepdims=True)

    for rel, stage in order:
        sib_copy(rel, stage).wait_send()
    for way in (0, 1):
        for stage in (0, 1):
            far_copy(way, stage).wait_send()
            agf_copy(way, stage).wait_send()
        for quarter in range(4):
            near_copy(way, quarter).wait_send()
            ag_copy(way, quarter).wait_send()
    for j in range(mats):

        @pl.when(f != owners[j])
        def _():
            in_copy(j).wait_send()

    @pl.when(is_owner)
    def _():
        def one(step, carry):
            slot = (slot_here + step) % shards
            out_copy(slot % y_size, slot // y_size).wait_send()
            return carry

        lax.fori_loop(1, shards, one, 0)

    for j in range(mats):
        here = block(out_ref, j)
        pltpu.make_async_copy(here, here, out_recv.at[j]).wait()


def body(gradients, row_counts, domain_ids, domain_weights):
    groups = lax.axis_size("domain")
    shards = lax.axis_size("fsdp")
    matrices, height, width = gradients.shape[1:]
    mats = matrices // groups
    y_size = 4 if shards == 64 else 2
    z_size = shards // y_size
    sizes = (groups, y_size, z_size, mats, height, width)
    assert groups == CORES * RING
    block = lambda count: pltpu.VMEM((count * height, width), BF16)
    square = lambda dtype: pltpu.VMEM((width, width), dtype)
    dma = lambda *shape: pltpu.SemaphoreType.DMA(shape)
    red = groups + y_size + z_size
    finished, new_weights = pl.pallas_call(
        functools.partial(kernel, sizes),
        out_shape=(
            jax.ShapeDtypeStruct((mats * height, width), BF16),
            jax.ShapeDtypeStruct((1, 128), F32),
        ),
        in_specs=[pl.BlockSpec(memory_space=pltpu.SMEM)] * 3
        + [pl.BlockSpec(memory_space=pl.ANY)],
        out_specs=(
            pl.BlockSpec(memory_space=pl.ANY),
            pl.BlockSpec(memory_space=pltpu.VMEM),
        ),
        scratch_shapes=[
            block(RING * mats), block(RING * mats), block(mats), block(2 * mats),
            block(mats), block(2 * mats), block(RING * mats), block(shards), block(shards),
            square(F32), square(F32), square(F32), square(F32),
            square(BF16), square(BF16), square(BF16), square(BF16),
            pltpu.VMEM((red, 8, 128), F32), pltpu.VMEM((8, width), F32),
            dma(4, 2), dma(4, 2), dma(4, 2), dma(4), dma(4), dma(2, 4), dma(2, 4),
            dma(2, 4), dma(2, 4), dma(2, 2), dma(2, 2), dma(mats), dma(z_size),
            dma(shards), dma(mats), dma(red), dma(red),
        ],
        compiler_params=pltpu.CompilerParams(
            collective_id=0, has_side_effects=True, vmem_limit_bytes=48 * 2**20
        ),
        cost_estimate=pl.CostEstimate(
            flops=20 * 10**9, bytes_accessed=8 * 2**20, transcendentals=0
        ),
    )(row_counts, domain_ids, domain_weights, gradients.reshape(matrices * height, width))
    full_rows = height * shards
    updates = finished.reshape(mats, height, width).astype(F32) * (
        MUON_SCALE * math.sqrt(full_rows)
    )
    return (updates, new_weights[0, :groups])


def solution(mesh):
    placed = (P("domain", None, "fsdp", None), P(), P(), P())
    return jax.shard_map(
        body,
        mesh=mesh,
        in_specs=placed,
        out_specs=(P("domain", "fsdp", None), P()),
        check_vma=False,
    )
```

```python
import functools
import math

import jax
import jax.numpy as jnp
from jax import lax
from jax.experimental import pallas as pl
from jax.experimental.pallas import tpu as pltpu
from jax.sharding import PartitionSpec as P

COEF_A = 3.4445
COEF_B = -4.775
COEF_C = 2.0315
MUON_SCALE = 0.2
ETA = 4.0
F32 = jnp.float32
BF16 = jnp.bfloat16
CORES = 2
RING = 4


def owner_position(slot, core, y_size, z_size):
    if y_size * z_size != 64:
        return CORES * slot + core
    quad, half = slot % 4, slot // 4
    z_pos = 4 * quad + 2 * half + core
    y_pos = (quad + ((0, 2), (1, 0))[half][core]) % 4
    return y_pos * z_size + z_pos


def kernel(
    sizes,
    counts_ref, ids_ref, weights_ref, grads_ref,
    out_ref, new_ref,
    own, sib, far_out, near_out, far_in, near_in, comb, rows, done,
    gram, gram_in, term, lin0, lin1, gram_b, term_b, lin0_b, lin1_b, score, sq_acc,
    own_sem, sib_send, sib_recv, far_send, far_recv, near_send, near_recv,
    ag_send, ag_recv, agf_send, agf_recv, in_send, in_recv, out_send, out_recv,
    red_send, red_recv, swap_send, swap_recv, known,
):
    groups, y_size, z_size, z_low, mats, height, width = sizes
    z_high = z_size // z_low
    bands = z_size // CORES
    pair = mats // 4
    d = lax.axis_index("domain")
    f = lax.axis_index("fsdp")
    x, core = d // CORES, d % CORES
    y, z = f // z_size, f % z_size
    zh, zl = z // z_low, z % z_low
    sibling = CORES * x + (1 - core)
    ring = [(x + step) % RING for step in (2, 1, 3, 0)]
    plus, minus = CORES * ring[1] + core, CORES * ring[2] + core
    def owner(j, of_core):
        return jnp.where(
            of_core == 0,
            owner_position(j, 0, y_size, z_size),
            owner_position(j, 1, y_size, z_size),
        )

    owners = [owner(j, core) for j in range(mats)]
    own_slot = jnp.int32(0)
    owned = jnp.int32(0)
    role = jnp.int32(0)
    for j in range(mats):
        first, second = f == owners[j], f == owner(j, 1 - core)
        either = jnp.logical_or(first, second)
        own_slot = jnp.where(either, j, own_slot)
        owned = jnp.where(either, 1, owned)
        role = jnp.where(second, 1, role)
    is_owner = owned == 1
    owned_block = jnp.where(role == 0, d, CORES * x + (1 - core))

    def remote(src, dst, send, recv, dd, ff):
        return pltpu.make_async_remote_copy(
            src_ref=src, dst_ref=dst, send_sem=send, recv_sem=recv,
            device_id=(dd, ff), device_id_type=pl.DeviceIdType.MESH,
        )

    def block(ref, first, count=1):
        return ref.at[pl.ds(first * height, count * height)]

    barrier = pltpu.get_barrier_semaphore()

    def greet(dd, ff):
        pl.semaphore_signal(
            barrier, inc=1, device_id=(dd, ff), device_id_type=pl.DeviceIdType.MESH
        )

    half = mats // 2

    def own_copy(rel, stage):
        first = mats * (CORES * ring[rel] + core) + half * stage
        return pltpu.make_async_copy(
            block(grads_ref, first, half),
            block(own, rel * mats + half * stage, half),
            own_sem.at[rel, stage],
        )

    def sib_copy(rel, stage):
        first = mats * (CORES * ring[rel] + (1 - core)) + half * stage
        return remote(
            block(grads_ref, first, half),
            block(sib, rel * mats + half * stage, half),
            sib_send.at[rel, stage], sib_recv.at[rel, stage], sibling, f,
        )

    order = [(0, 0), (1, 0), (2, 0), (0, 1), (3, 0), (1, 1), (2, 1), (3, 1)]
    for rel, stage in order:
        own_copy(rel, stage).start()

    def at_y(step):
        return d, (y + step) % y_size * z_size + z

    def at_low(step):
        return d, y * z_size + zh * z_low + (zl + step) % z_low

    def at_high(step):
        return d, y * z_size + (zh + step) % z_high * z_low + zl

    def at_x(step):
        return CORES * ((x + step) % RING) + core, f

    greet(sibling, f)
    for size, where in ((RING, at_x), (y_size, at_y), (z_low, at_low), (z_high, at_high)):
        for step in range(1, size):
            greet(*where(step))
    pl.semaphore_wait(barrier, 1 + (RING - 1) + (y_size - 1) + (z_low - 1) + (z_high - 1))

    relays = ((z_high, at_high), (y_size, at_y), (2, lambda step: (sibling, f)))

    def tell(stage):
        size, where = relays[stage]
        for step in range(1, size):
            dd, ff = where(step)
            pl.semaphore_signal(
                known.at[stage], inc=1, device_id=(dd, ff),
                device_id_type=pl.DeviceIdType.MESH,
            )

    def hear(stage):
        pl.semaphore_wait(known.at[stage], relays[stage][0] - 1)

    tell(0)
    for rel, stage in order:
        sib_copy(rel, stage).start()

    total_weight = weights_ref[0]
    for k in range(1, groups):
        total_weight = total_weight + weights_ref[k]

    def mix_row(group):
        kind = ids_ref[group]
        count = jnp.float32(0)
        for h in range(groups):
            count = count + jnp.where(ids_ref[h] == kind, 1.0, 0.0)
        full = lambda value: jnp.full((1, width), value, F32)
        return full(weights_ref[kind]) / full(total_weight) / jnp.maximum(full(count), 1.0)

    mix_own, mix_sib = mix_row(d), mix_row(sibling)

    def keep(rel, j):
        index = mats * (CORES * ring[rel] + core) + j
        return jnp.where(f * height < counts_ref[index], 1.0, 0.0)

    def partial(rel, j):
        at = pl.ds((rel * mats + j) * height, height)
        kept = keep(rel, j)
        return (mix_own * kept) * own[at, :].astype(F32) + (mix_sib * kept) * sib[
            at, :
        ].astype(F32)

    def arrived(rel, stage):
        own_copy(rel, stage).wait()
        sib_copy(rel, stage).wait_recv()

    def far_copy(way, stage):
        part = way * 2 + stage
        return remote(
            block(far_out, part * pair, pair), block(far_in, part * pair, pair),
            far_send.at[part], far_recv.at[part], (plus, minus)[way], f,
        )

    def near_copy(way, quarter):
        first = way * mats + quarter * pair
        return remote(
            block(near_out, first, pair), block(near_in, first, pair),
            near_send.at[way, quarter], near_recv.at[way, quarter], (plus, minus)[way], f,
        )

    def send_far(stage):
        arrived(0, stage)
        for way in (0, 1):
            for i in range(pair):
                at = pl.ds(((way * 2 + stage) * pair + i) * height, height)
                far_out[at, :] = partial(0, (2 * stage + way) * pair + i).astype(BF16)
            far_copy(way, stage).start()

    def send_near(stage):
        for way in (0, 1):
            arrived(1 + way, stage)
            quarter = 2 * stage + 1 - way
            for i in range(pair):
                j = quarter * pair + i
                at = pl.ds((way * mats + j) * height, height)
                near_out[at, :] = partial(1 + way, j).astype(BF16)
            near_copy(way, quarter).start()

    def send_merged(stage):
        for way in (0, 1):
            far_copy(way, stage).wait_recv()
            quarter = 2 * stage + way
            for i in range(pair):
                j = quarter * pair + i
                at = pl.ds((way * mats + j) * height, height)
                came = pl.ds(((way * 2 + stage) * pair + i) * height, height)
                near_out[at, :] = (
                    partial(1 + way, j) + far_in[came, :].astype(F32)
                ).astype(BF16)
            near_copy(way, quarter).start()

    odd = z % CORES
    slot_here = z // CORES * y_size + y

    def in_copy(j):
        return remote(
            block(comb, 3 * mats + j), block(rows, slot_here),
            in_send.at[j], in_recv.at[z // CORES],
            jnp.where(odd == 0, d, sibling), owners[j],
        )

    def stays(j):
        return jnp.logical_and(f == owners[j], odd == 0)

    def combine(stage):
        arrived(3, stage)
        for quarter in (2 * stage, 2 * stage + 1):
            for way in (0, 1):
                near_copy(way, quarter).wait_recv()
            for i in range(pair):
                j = quarter * pair + i
                left = pl.ds(j * height, height)
                right = pl.ds((mats + j) * height, height)
                value = partial(3, j) + (
                    near_in[left, :].astype(F32) + near_in[right, :].astype(F32)
                )
                sq_acc[...] += jnp.sum(
                    (value * value).reshape(height // 8, 8, width), axis=0
                )
                comb[pl.ds((3 * mats + j) * height, height), :] = value.astype(BF16)

                @pl.when(jnp.logical_not(stays(j)))
                def _():
                    in_copy(j).start()

                @pl.when(stays(j))
                def _():
                    pltpu.make_async_copy(
                        block(comb, 3 * mats + j), block(rows, slot_here),
                        in_recv.at[z // CORES],
                    ).start()

    sq_acc[...] = jnp.zeros_like(sq_acc)
    send_far(0)
    hear(0)
    tell(1)
    send_near(0)
    hear(1)
    tell(2)
    send_far(1)
    send_merged(0)
    send_near(1)
    hear(2)
    combine(0)
    send_merged(1)
    combine(1)

    def ag_copy(way, quarter):
        first = quarter * pair
        return remote(
            block(comb, 3 * mats + first, pair),
            block(comb, (2, 1)[way] * mats + first, pair),
            ag_send.at[way, quarter], ag_recv.at[way, quarter], (plus, minus)[way], f,
        )

    def agf_copy(way, stage):
        first = (2 * stage + way) * pair
        return remote(
            block(comb, (2, 1)[way] * mats + first, pair), block(comb, first, pair),
            agf_send.at[way, stage], agf_recv.at[way, stage], (plus, minus)[way], f,
        )

    for quarter in range(4):
        for way in (0, 1):
            ag_copy(way, quarter).start()

    band = y_size * height

    def near_band(step):
        shift = jnp.where(step % 2 == 1, (step + 1) // 2, bands - step // 2)
        return (z // CORES + shift) % bands

    swap = remote(gram, gram_in, swap_send, swap_recv, sibling, f)

    @pl.when(is_owner)
    def _():
        gram[...] = jnp.zeros_like(gram)

        def one(step, carry):
            index = near_band(step)
            here = rows.at[pl.ds(index * band, band)]
            pltpu.make_async_copy(here, here, in_recv.at[index]).wait()
            part = here[...]
            gram[...] += lax.dot_general(
                part, part, (((0,), (0,)), ((), ())), preferred_element_type=F32
            )
            return carry

        lax.fori_loop(0, bands, one, 0)
        swap.start()

    for stage in (0, 1):
        for way in (0, 1):
            ag_copy(way, 2 * stage + way).wait_recv()
            agf_copy(way, stage).start()

    def out_place(index, y_to):
        return y_to * z_size + CORES * index + role

    def out_stays(index, y_to):
        return jnp.logical_and(role == 0, out_place(index, y_to) == f)

    def out_copy(index, y_to):
        slot = index * y_size + y_to
        return remote(
            block(done, slot), block(out_ref, own_slot),
            out_send.at[slot], out_recv.at[own_slot],
            owned_block, out_place(index, y_to),
        )

    @pl.when(is_owner)
    def _():
        row_id = lax.broadcasted_iota(jnp.int32, (width, width), 0)
        col_id = lax.broadcasted_iota(jnp.int32, (width, width), 1)
        swap.wait_recv()
        gram_in[...] += gram[...]
        swap.wait_send()
        trace = jnp.sum(
            jnp.where(row_id == col_id, gram_in[...], 0.0), axis=0, keepdims=True
        )
        trace = jnp.sum(trace, axis=1, keepdims=True)
        scale = 1.0 / (jnp.sqrt(trace) + 1e-07)
        dot = lambda a, b: jnp.dot(a[...], b[...], preferred_element_type=F32)

        gram[...] = gram_in[...] * scale * scale
        gram_b[...] = gram[...].astype(BF16)
        for lin, lin_b in ((lin0, lin0_b), (lin1, lin1_b)):
            lin[...] = COEF_B * gram[...] + COEF_C * dot(gram_b, gram_b)
            lin_b[...] = lin[...].astype(BF16)
            term[...] = COEF_A * gram[...] + dot(lin_b, gram_b)
            term_b[...] = term[...].astype(BF16)
            gram[...] = COEF_A * term[...] + dot(lin_b, term_b)
            gram_b[...] = gram[...].astype(BF16)
        lin0[...] = COEF_A * (lin0[...] + lin1[...]) + dot(lin0_b, lin1_b)
        lin0_b[...] = lin0[...].astype(BF16)
        lin1[...] = COEF_B * gram[...] + COEF_C * dot(gram_b, gram_b)
        lin1_b[...] = lin1[...].astype(BF16)
        whole = COEF_A**2 * lin1[...] + COEF_A * lin0[...] + dot(lin0_b, lin1_b)
        whole = whole + jnp.where(row_id == col_id, COEF_A**3, 0.0)
        gram_b[...] = (whole * scale).astype(BF16)

        def one(step, carry):
            index = near_band(bands - 1 - step)
            at = pl.ds(index * band, band)
            done[at, :] = jnp.dot(
                rows[at, :], gram_b[...], preferred_element_type=F32
            ).astype(BF16)
            for y_to in range(y_size):
                here = out_stays(index, y_to)

                @pl.when(jnp.logical_not(here))
                def _():
                    out_copy(index, y_to).start()

                @pl.when(here)
                def _():
                    pltpu.make_async_copy(
                        block(done, index * y_size + y_to), block(out_ref, own_slot),
                        out_recv.at[own_slot],
                    ).start()

            return carry

        lax.fori_loop(0, bands, one, 0)

    for way in (0, 1):
        for quarter in range(4):
            if quarter % 2 != way:
                ag_copy(way, quarter).wait_recv()
        for stage in (0, 1):
            agf_copy(way, stage).wait_recv()

    fold = lambda value: jnp.sum(value.reshape(height // 8, 8, width), axis=0)

    def align(index, carry):
        rel, j = index // mats, index % mats
        step = jnp.where(rel == 0, 2, jnp.where(rel == 1, 1, jnp.where(rel == 2, 3, 0)))
        matrix = mats * (CORES * ((x + step) % RING) + core) + j
        kept = jnp.where(f * height < counts_ref[matrix], 1.0, 0.0)
        at = pl.ds(index * height, height)
        mine, other = own[at, :].astype(F32), sib[at, :].astype(F32)
        both = comb[at, :].astype(F32)
        return (
            carry[0] + fold(mine * both),
            carry[1] + fold(other * both),
            carry[2] + kept * fold(mine * mine),
            carry[3] + kept * fold(other * other),
        )

    empty = jnp.zeros((8, width), F32)
    sums = lax.fori_loop(0, RING * mats, align, (empty,) * 4)
    sums = [
        jnp.sum(jnp.sum(value, axis=0, keepdims=True), axis=1, keepdims=True)
        for value in (*sums, sq_acc[...])
    ]
    sub = lax.broadcasted_iota(jnp.int32, (8, 128), 0)
    lane = lax.broadcasted_iota(jnp.int32, (8, 128), 1)

    def by_group(mine, other):
        return jnp.where(sub == d, mine, jnp.where(sub == sibling, other, 0.0))

    tile = jnp.where(
        lane == 0,
        by_group(sums[0], sums[1]),
        jnp.where(
            lane == 1,
            by_group(sums[2], sums[3]),
            jnp.where(lane == 2, sums[4], 0.0),
        ),
    )
    base = 0
    for size, place, where in (
        (2, core, lambda step: (sibling, f)),
        (RING, x, at_x),
        (y_size, y, at_y),
        (z_low, zl, at_low),
        (z_high, zh, at_high),
    ):
        score[base + place] = tile

        def red_copy(step, base=base, size=size, place=place, where=where):
            return remote(
                score.at[base + place], score.at[base + place],
                red_send.at[base + step], red_recv.at[base + place],
                *where(step),
            )

        def red_wait(step, base=base, size=size, place=place):
            came = score.at[base + (place + step) % size]
            pltpu.make_async_copy(
                came, came, red_recv.at[base + (place + step) % size]
            ).wait()

        for step in range(1, size):
            red_copy(step).start()
        for step in range(1, size):
            red_wait(step)
        tile = score[base]
        for i in range(1, size):
            tile = tile + score[base + i]
        for step in range(1, size):
            red_copy(step).wait_send()
        base += size

    id_col = jnp.zeros((8, 128), jnp.int32)
    weight_row = jnp.zeros((1, 128), F32)
    for g in range(groups):
        id_col = jnp.where(sub == g, ids_ref[g], id_col)
        weight_row = jnp.where(lane[:1] == g, weights_ref[g], weight_row)
    column = lambda k: jnp.sum(jnp.where(lane == k, tile, 0.0), axis=1, keepdims=True)
    aligned, squares, total_sq = column(0), column(1), column(2)
    cosine = aligned / (jnp.sqrt(squares) * jnp.sqrt(total_sq) + 1e-06)
    onehot = jnp.where(id_col == lane, 1.0, 0.0)
    kind_counts = jnp.sum(onehot, axis=0, keepdims=True)
    points = jnp.sum(onehot * cosine, axis=0, keepdims=True) / jnp.maximum(kind_counts, 1.0)
    share = weight_row / jnp.full((1, 128), total_weight, F32)
    raised = share * jnp.exp(ETA * points)
    new_ref[...] = raised / jnp.sum(raised, axis=1, keepdims=True)

    for rel, stage in order:
        sib_copy(rel, stage).wait_send()
    for way in (0, 1):
        for stage in (0, 1):
            far_copy(way, stage).wait_send()
            agf_copy(way, stage).wait_send()
        for quarter in range(4):
            near_copy(way, quarter).wait_send()
            ag_copy(way, quarter).wait_send()
    for j in range(mats):

        @pl.when(jnp.logical_not(stays(j)))
        def _():
            in_copy(j).wait_send()

    @pl.when(is_owner)
    def _():
        def one(index, carry):
            for y_to in range(y_size):

                @pl.when(jnp.logical_not(out_stays(index, y_to)))
                def _():
                    out_copy(index, y_to).wait_send()

            return carry

        lax.fori_loop(0, bands, one, 0)

    for j in range(mats):
        here = block(out_ref, j)
        pltpu.make_async_copy(here, here, out_recv.at[j]).wait()


def body(gradients, row_counts, domain_ids, domain_weights):
    groups = lax.axis_size("domain")
    shards = lax.axis_size("fsdp")
    matrices, height, width = gradients.shape[1:]
    mats = matrices // groups
    y_size = 4 if shards == 64 else 2
    z_size = shards // y_size
    z_low = 4 if z_size == 16 else 2
    sizes = (groups, y_size, z_size, z_low, mats, height, width)
    assert groups == CORES * RING
    block = lambda count: pltpu.VMEM((count * height, width), BF16)
    square = lambda dtype: pltpu.VMEM((width, width), dtype)
    dma = lambda *shape: pltpu.SemaphoreType.DMA(shape)
    red = CORES + RING + y_size + z_low + z_size // z_low
    held = shards // CORES
    finished, new_weights = pl.pallas_call(
        functools.partial(kernel, sizes),
        out_shape=(
            jax.ShapeDtypeStruct((mats * height, width), BF16),
            jax.ShapeDtypeStruct((1, 128), F32),
        ),
        in_specs=[pl.BlockSpec(memory_space=pltpu.SMEM)] * 3
        + [pl.BlockSpec(memory_space=pl.ANY)],
        out_specs=(
            pl.BlockSpec(memory_space=pl.ANY),
            pl.BlockSpec(memory_space=pltpu.VMEM),
        ),
        scratch_shapes=[
            block(RING * mats), block(RING * mats), block(mats), block(2 * mats),
            block(mats), block(2 * mats), block(RING * mats), block(held), block(held),
            *[square(F32)] * 5,
            *[square(BF16)] * 4,
            pltpu.VMEM((red, 8, 128), F32), pltpu.VMEM((8, width), F32),
            dma(4, 2), dma(4, 2), dma(4, 2), dma(4), dma(4), dma(2, 4), dma(2, 4),
            dma(2, 4), dma(2, 4), dma(2, 2), dma(2, 2), dma(mats), dma(z_size // CORES),
            dma(held), dma(mats), dma(red), dma(red), pltpu.SemaphoreType.DMA,
            pltpu.SemaphoreType.DMA, pltpu.SemaphoreType.REGULAR((3,)),
        ],
        compiler_params=pltpu.CompilerParams(
            collective_id=0, has_side_effects=True, vmem_limit_bytes=60 * 2**20
        ),
        cost_estimate=pl.CostEstimate(
            flops=20 * 10**9, bytes_accessed=8 * 2**20, transcendentals=0
        ),
    )(row_counts, domain_ids, domain_weights, gradients.reshape(matrices * height, width))
    full_rows = height * shards
    updates = finished.reshape(mats, height, width).astype(F32) * (
        MUON_SCALE * math.sqrt(full_rows)
    )
    return (updates, new_weights[0, :groups])


def solution(mesh):
    placed = (P("domain", None, "fsdp", None), P(), P(), P())
    return jax.shard_map(
        body,
        mesh=mesh,
        in_specs=placed,
        out_specs=(P("domain", "fsdp", None), P()),
        check_vma=False,
    )
```

```python
import functools
import math

import jax
import jax.numpy as jnp
from jax import lax
from jax.experimental import pallas as pl
from jax.experimental.pallas import tpu as pltpu
from jax.sharding import PartitionSpec as P

COEF_A = 3.4445
COEF_B = -4.775
COEF_C = 2.0315
MUON_SCALE = 0.2
ETA = 4.0
F32 = jnp.float32
BF16 = jnp.bfloat16
CORES = 2
RING = 4


def owner_position(slot, core, y_size, z_size):
    if y_size * z_size != 64:
        return CORES * slot + core
    z_pos = slot % 4 + 4 * (slot // 4) + 8 * core
    return slot % 4 * z_size + z_pos


def kernel(
    sizes,
    counts_ref, ids_ref, weights_ref, grads_ref,
    out_ref, new_ref,
    own, sib, far_out, near_out, far_in, near_in, comb, rows, done,
    gram, gram_in, term, lin0, lin1, gram_b, term_b, lin0_b, lin1_b, score, sq_acc,
    own_sem, sib_send, sib_recv, far_send, far_recv, near_send, near_recv,
    ag_send, ag_recv, in_send, in_recv, out_send, out_recv,
    red_send, red_recv, swap_send, swap_recv, known,
):
    groups, y_size, z_size, z_low, mats, height, width = sizes
    z_high = z_size // z_low
    bands = z_size // CORES
    pair = mats // 4
    d = lax.axis_index("domain")
    f = lax.axis_index("fsdp")
    x, core = d // CORES, d % CORES
    y, z = f // z_size, f % z_size
    zh, zl = z // z_low, z % z_low
    sibling = CORES * x + (1 - core)
    ring = [(x + step) % RING for step in (2, 1, 3, 0)]
    plus, minus = CORES * ring[1] + core, CORES * ring[2] + core
    def owner(j, of_core):
        return jnp.where(
            of_core == 0,
            owner_position(j, 0, y_size, z_size),
            owner_position(j, 1, y_size, z_size),
        )

    own_slot = jnp.int32(0)
    owned = jnp.int32(0)
    role = jnp.int32(0)
    for j in range(mats):
        first, second = f == owner(j, core), f == owner(j, 1 - core)
        either = jnp.logical_or(first, second)
        own_slot = jnp.where(either, j, own_slot)
        owned = jnp.where(either, 1, owned)
        role = jnp.where(second, 1, role)
    is_owner = owned == 1
    owned_block = jnp.where(role == 0, d, CORES * x + (1 - core))

    def remote(src, dst, send, recv, dd, ff):
        return pltpu.make_async_remote_copy(
            src_ref=src, dst_ref=dst, send_sem=send, recv_sem=recv,
            device_id=(dd, ff), device_id_type=pl.DeviceIdType.MESH,
        )

    def block(ref, first, count=1):
        return ref.at[pl.ds(first * height, count * height)]

    barrier = pltpu.get_barrier_semaphore()

    def greet(dd, ff):
        pl.semaphore_signal(
            barrier, inc=1, device_id=(dd, ff), device_id_type=pl.DeviceIdType.MESH
        )

    half = mats // 2

    def own_copy(rel, stage):
        first = mats * (CORES * ring[rel] + core) + half * stage
        return pltpu.make_async_copy(
            block(grads_ref, first, half),
            block(own, rel * mats + half * stage, half),
            own_sem.at[rel, stage],
        )

    def sib_copy(rel, stage):
        first = mats * (CORES * ring[rel] + (1 - core)) + half * stage
        return remote(
            block(grads_ref, first, half),
            block(sib, rel * mats + half * stage, half),
            sib_send.at[rel, stage], sib_recv.at[rel, stage], sibling, f,
        )

    order = [(0, 0), (1, 0), (2, 0), (0, 1), (3, 0), (1, 1), (2, 1), (3, 1)]
    for rel, stage in order:
        own_copy(rel, stage).start()

    def at_y(step):
        return d, (y + step) % y_size * z_size + z

    def at_low(step):
        return d, y * z_size + zh * z_low + (zl + step) % z_low

    def at_high(step):
        return d, y * z_size + (zh + step) % z_high * z_low + zl

    def at_x(step):
        return CORES * ((x + step) % RING) + core, f

    greet(sibling, f)
    for size, where in ((RING, at_x), (y_size, at_y), (z_low, at_low), (z_high, at_high)):
        for step in range(1, size):
            greet(*where(step))
    pl.semaphore_wait(barrier, 1 + (RING - 1) + (y_size - 1) + (z_low - 1) + (z_high - 1))

    relays = ((z_high, at_high), (y_size, at_y), (2, lambda step: (sibling, f)))

    def tell(stage):
        size, where = relays[stage]
        for step in range(1, size):
            dd, ff = where(step)
            pl.semaphore_signal(
                known.at[stage], inc=1, device_id=(dd, ff),
                device_id_type=pl.DeviceIdType.MESH,
            )

    def hear(stage):
        pl.semaphore_wait(known.at[stage], relays[stage][0] - 1)

    tell(0)
    for rel, stage in order:
        sib_copy(rel, stage).start()

    total_weight = weights_ref[0]
    for k in range(1, groups):
        total_weight = total_weight + weights_ref[k]

    def mix_row(group):
        kind = ids_ref[group]
        count = jnp.float32(0)
        for h in range(groups):
            count = count + jnp.where(ids_ref[h] == kind, 1.0, 0.0)
        full = lambda value: jnp.full((1, width), value, F32)
        return full(weights_ref[kind]) / full(total_weight) / jnp.maximum(full(count), 1.0)

    mix_own, mix_sib = mix_row(d), mix_row(sibling)

    def keep(rel, j):
        index = mats * (CORES * ring[rel] + core) + j
        return jnp.where(f * height < counts_ref[index], 1.0, 0.0)

    def partial(rel, j):
        at = pl.ds((rel * mats + j) * height, height)
        kept = keep(rel, j)
        return (mix_own * kept) * own[at, :].astype(F32) + (mix_sib * kept) * sib[
            at, :
        ].astype(F32)

    def arrived(rel, stage):
        own_copy(rel, stage).wait()
        sib_copy(rel, stage).wait_recv()

    def far_copy(way, stage):
        part = way * 2 + stage
        return remote(
            block(far_out, part * pair, pair), block(far_in, part * pair, pair),
            far_send.at[part], far_recv.at[part], (plus, minus)[way], f,
        )

    def near_copy(way, quarter):
        first = way * mats + quarter * pair
        return remote(
            block(near_out, first, pair), block(near_in, first, pair),
            near_send.at[way, quarter], near_recv.at[way, quarter], (plus, minus)[way], f,
        )

    def send_far(stage):
        arrived(0, stage)
        for way in (0, 1):
            for i in range(pair):
                at = pl.ds(((way * 2 + stage) * pair + i) * height, height)
                far_out[at, :] = partial(0, (2 * stage + way) * pair + i).astype(BF16)
            far_copy(way, stage).start()

    def send_near(stage):
        for way in (0, 1):
            arrived(1 + way, stage)
            quarter = 2 * stage + 1 - way
            for i in range(pair):
                j = quarter * pair + i
                at = pl.ds((way * mats + j) * height, height)
                near_out[at, :] = partial(1 + way, j).astype(BF16)
            near_copy(way, quarter).start()

    def send_merged(stage):
        for way in (0, 1):
            far_copy(way, stage).wait_recv()
            quarter = 2 * stage + way
            for i in range(pair):
                j = quarter * pair + i
                at = pl.ds((way * mats + j) * height, height)
                came = pl.ds(((way * 2 + stage) * pair + i) * height, height)
                near_out[at, :] = (
                    partial(1 + way, j) + far_in[came, :].astype(F32)
                ).astype(BF16)
            near_copy(way, quarter).start()

    odd = z % CORES
    slot_here = z // CORES * y_size + y

    def in_copy(j):
        return remote(
            block(comb, 3 * mats + j), block(rows, slot_here),
            in_send.at[j], in_recv.at[z // CORES],
            jnp.where(odd == 0, d, sibling), owner(j, core),
        )

    def stays(j):
        return jnp.logical_and(f == owner(j, core), odd == 0)

    def combine(stage):
        arrived(3, stage)
        for quarter in (2 * stage, 2 * stage + 1):
            for way in (0, 1):
                near_copy(way, quarter).wait_recv()
            for i in range(pair):
                j = quarter * pair + i
                left = pl.ds(j * height, height)
                right = pl.ds((mats + j) * height, height)
                value = partial(3, j) + (
                    near_in[left, :].astype(F32) + near_in[right, :].astype(F32)
                )
                sq_acc[...] += jnp.sum(
                    (value * value).reshape(height // 8, 8, width), axis=0
                )
                comb[pl.ds((3 * mats + j) * height, height), :] = value.astype(BF16)
        for i in range(half):
            j = half * stage + (i + z + y) % half

            @pl.when(jnp.logical_not(stays(j)))
            def _():
                in_copy(j).start()

            @pl.when(stays(j))
            def _():
                pltpu.make_async_copy(
                    block(comb, 3 * mats + j), block(rows, slot_here),
                    in_recv.at[z // CORES],
                ).start()

    def ag_copy(step, stage):
        first = half * stage
        return remote(
            block(comb, 3 * mats + first, half),
            block(comb, (3, 2, 0, 1)[step] * mats + first, half),
            ag_send.at[step, stage], ag_recv.at[step, stage], *at_x(step),
        )

    def gather(stage):
        for step in range(1, RING):
            ag_copy(step, stage).start()

    sq_acc[...] = jnp.zeros_like(sq_acc)
    send_far(0)
    hear(0)
    tell(1)
    send_near(0)
    hear(1)
    tell(2)
    send_far(1)
    send_merged(0)
    send_near(1)
    hear(2)
    combine(0)
    send_merged(1)
    gather(0)
    combine(1)
    gather(1)

    band = y_size * height

    def near_band(step):
        shift = jnp.where(step % 2 == 1, (step + 1) // 2, bands - step // 2)
        return (z // CORES + shift) % bands

    swap = remote(gram, gram_in, swap_send, swap_recv, sibling, f)

    @pl.when(is_owner)
    def _():
        gram[...] = jnp.zeros_like(gram)

        def one(step, carry):
            index = near_band(step)
            here = rows.at[pl.ds(index * band, band)]
            pltpu.make_async_copy(here, here, in_recv.at[index]).wait()
            part = here[...]
            gram[...] += lax.dot_general(
                part, part, (((0,), (0,)), ((), ())), preferred_element_type=F32
            )
            return carry

        lax.fori_loop(0, bands, one, 0)
        swap.start()

    def out_place(index, y_to):
        return y_to * z_size + CORES * index + role

    def out_stays(index, y_to):
        return jnp.logical_and(role == 0, out_place(index, y_to) == f)

    def out_copy(index, y_to):
        slot = index * y_size + y_to
        return remote(
            block(done, slot), block(out_ref, own_slot),
            out_send.at[slot], out_recv.at[own_slot],
            owned_block, out_place(index, y_to),
        )

    @pl.when(is_owner)
    def _():
        row_id = lax.broadcasted_iota(jnp.int32, (width, width), 0)
        col_id = lax.broadcasted_iota(jnp.int32, (width, width), 1)
        swap.wait_recv()
        gram_in[...] += gram[...]
        swap.wait_send()
        trace = jnp.sum(
            jnp.where(row_id == col_id, gram_in[...], 0.0), axis=0, keepdims=True
        )
        trace = jnp.sum(trace, axis=1, keepdims=True)
        scale = 1.0 / (jnp.sqrt(trace) + 1e-07)
        dot = lambda a, b: jnp.dot(a[...], b[...], preferred_element_type=F32)

        gram[...] = gram_in[...] * scale * scale
        gram_b[...] = gram[...].astype(BF16)
        for lin, lin_b in ((lin0, lin0_b), (lin1, lin1_b)):
            lin[...] = COEF_B * gram[...] + COEF_C * dot(gram_b, gram_b)
            lin_b[...] = lin[...].astype(BF16)
            term[...] = COEF_A * gram[...] + dot(lin_b, gram_b)
            term_b[...] = term[...].astype(BF16)
            gram[...] = COEF_A * term[...] + dot(lin_b, term_b)
            gram_b[...] = gram[...].astype(BF16)
        lin0[...] = COEF_A * (lin0[...] + lin1[...]) + dot(lin0_b, lin1_b)
        lin0_b[...] = lin0[...].astype(BF16)
        lin1[...] = COEF_B * gram[...] + COEF_C * dot(gram_b, gram_b)
        lin1_b[...] = lin1[...].astype(BF16)
        whole = COEF_A**2 * lin1[...] + COEF_A * lin0[...] + dot(lin0_b, lin1_b)
        whole = whole + jnp.where(row_id == col_id, COEF_A**3, 0.0)
        gram_b[...] = (whole * scale).astype(BF16)

        def one(step, carry):
            index = near_band(bands - 1 - step)
            at = pl.ds(index * band, band)
            done[at, :] = jnp.dot(
                rows[at, :], gram_b[...], preferred_element_type=F32
            ).astype(BF16)
            for y_to in range(y_size):
                here = out_stays(index, y_to)

                @pl.when(jnp.logical_not(here))
                def _():
                    out_copy(index, y_to).start()

                @pl.when(here)
                def _():
                    pltpu.make_async_copy(
                        block(done, index * y_size + y_to), block(out_ref, own_slot),
                        out_recv.at[own_slot],
                    ).start()

            return carry

        lax.fori_loop(0, bands, one, 0)

    for stage in (0, 1):
        for step in range(1, RING):
            ag_copy(step, stage).wait_recv()

    fold = lambda value: jnp.sum(value.reshape(height // 8, 8, width), axis=0)

    def align(index, carry):
        rel, j = index // mats, index % mats
        step = jnp.where(rel == 0, 2, jnp.where(rel == 1, 1, jnp.where(rel == 2, 3, 0)))
        matrix = mats * (CORES * ((x + step) % RING) + core) + j
        kept = jnp.where(f * height < counts_ref[matrix], 1.0, 0.0)
        at = pl.ds(index * height, height)
        mine, other = own[at, :].astype(F32), sib[at, :].astype(F32)
        both = comb[at, :].astype(F32)
        return (
            carry[0] + fold(mine * both),
            carry[1] + fold(other * both),
            carry[2] + kept * fold(mine * mine),
            carry[3] + kept * fold(other * other),
        )

    empty = jnp.zeros((8, width), F32)
    sums = lax.fori_loop(0, RING * mats, align, (empty,) * 4)
    sums = [
        jnp.sum(jnp.sum(value, axis=0, keepdims=True), axis=1, keepdims=True)
        for value in (*sums, sq_acc[...])
    ]
    sub = lax.broadcasted_iota(jnp.int32, (8, 128), 0)
    lane = lax.broadcasted_iota(jnp.int32, (8, 128), 1)

    def by_group(mine, other):
        return jnp.where(sub == d, mine, jnp.where(sub == sibling, other, 0.0))

    tile = jnp.where(
        lane == 0,
        by_group(sums[0], sums[1]),
        jnp.where(
            lane == 1,
            by_group(sums[2], sums[3]),
            jnp.where(lane == 2, sums[4], 0.0),
        ),
    )
    base = 0
    for size, place, where in (
        (2, core, lambda step: (sibling, f)),
        (RING, x, at_x),
        (y_size, y, at_y),
        (z_low, zl, at_low),
        (z_high, zh, at_high),
    ):
        score[base + place] = tile

        def red_copy(step, base=base, size=size, place=place, where=where):
            return remote(
                score.at[base + place], score.at[base + place],
                red_send.at[base + step], red_recv.at[base + place],
                *where(step),
            )

        def red_wait(step, base=base, size=size, place=place):
            came = score.at[base + (place + step) % size]
            pltpu.make_async_copy(
                came, came, red_recv.at[base + (place + step) % size]
            ).wait()

        for step in range(1, size):
            red_copy(step).start()
        for step in range(1, size):
            red_wait(step)
        tile = score[base]
        for i in range(1, size):
            tile = tile + score[base + i]
        for step in range(1, size):
            red_copy(step).wait_send()
        base += size

    id_col = jnp.zeros((8, 128), jnp.int32)
    weight_row = jnp.zeros((1, 128), F32)
    for g in range(groups):
        id_col = jnp.where(sub == g, ids_ref[g], id_col)
        weight_row = jnp.where(lane[:1] == g, weights_ref[g], weight_row)
    column = lambda k: jnp.sum(jnp.where(lane == k, tile, 0.0), axis=1, keepdims=True)
    aligned, squares, total_sq = column(0), column(1), column(2)
    cosine = aligned / (jnp.sqrt(squares) * jnp.sqrt(total_sq) + 1e-06)
    onehot = jnp.where(id_col == lane, 1.0, 0.0)
    kind_counts = jnp.sum(onehot, axis=0, keepdims=True)
    points = jnp.sum(onehot * cosine, axis=0, keepdims=True) / jnp.maximum(kind_counts, 1.0)
    share = weight_row / jnp.full((1, 128), total_weight, F32)
    raised = share * jnp.exp(ETA * points)
    new_ref[...] = raised / jnp.sum(raised, axis=1, keepdims=True)

    for rel, stage in order:
        sib_copy(rel, stage).wait_send()
    for way in (0, 1):
        for stage in (0, 1):
            far_copy(way, stage).wait_send()
        for quarter in range(4):
            near_copy(way, quarter).wait_send()
    for stage in (0, 1):
        for step in range(1, RING):
            ag_copy(step, stage).wait_send()
    for j in range(mats):

        @pl.when(jnp.logical_not(stays(j)))
        def _():
            in_copy(j).wait_send()

    @pl.when(is_owner)
    def _():
        def one(index, carry):
            for y_to in range(y_size):

                @pl.when(jnp.logical_not(out_stays(index, y_to)))
                def _():
                    out_copy(index, y_to).wait_send()

            return carry

        lax.fori_loop(0, bands, one, 0)

    for j in range(mats):
        here = block(out_ref, j)
        pltpu.make_async_copy(here, here, out_recv.at[j]).wait()


def body(gradients, row_counts, domain_ids, domain_weights):
    groups = lax.axis_size("domain")
    shards = lax.axis_size("fsdp")
    matrices, height, width = gradients.shape[1:]
    mats = matrices // groups
    y_size = 4 if shards == 64 else 2
    z_size = shards // y_size
    z_low = 4 if z_size == 16 else 2
    sizes = (groups, y_size, z_size, z_low, mats, height, width)
    assert groups == CORES * RING
    block = lambda count: pltpu.VMEM((count * height, width), BF16)
    square = lambda dtype: pltpu.VMEM((width, width), dtype)
    dma = lambda *shape: pltpu.SemaphoreType.DMA(shape)
    red = CORES + RING + y_size + z_low + z_size // z_low
    held = shards // CORES
    finished, new_weights = pl.pallas_call(
        functools.partial(kernel, sizes),
        out_shape=(
            jax.ShapeDtypeStruct((mats * height, width), BF16),
            jax.ShapeDtypeStruct((1, 128), F32),
        ),
        in_specs=[pl.BlockSpec(memory_space=pltpu.SMEM)] * 3
        + [pl.BlockSpec(memory_space=pl.ANY)],
        out_specs=(
            pl.BlockSpec(memory_space=pl.ANY),
            pl.BlockSpec(memory_space=pltpu.VMEM),
        ),
        scratch_shapes=[
            block(RING * mats), block(RING * mats), block(mats), block(2 * mats),
            block(mats), block(2 * mats), block(RING * mats), block(held), block(held),
            *[square(F32)] * 5,
            *[square(BF16)] * 4,
            pltpu.VMEM((red, 8, 128), F32), pltpu.VMEM((8, width), F32),
            dma(4, 2), dma(4, 2), dma(4, 2), dma(4), dma(4), dma(2, 4), dma(2, 4),
            dma(4, 2), dma(4, 2), dma(mats), dma(z_size // CORES),
            dma(held), dma(mats), dma(red), dma(red), pltpu.SemaphoreType.DMA,
            pltpu.SemaphoreType.DMA, pltpu.SemaphoreType.REGULAR((3,)),
        ],
        compiler_params=pltpu.CompilerParams(
            collective_id=0, has_side_effects=True, vmem_limit_bytes=60 * 2**20
        ),
        cost_estimate=pl.CostEstimate(
            flops=20 * 10**9, bytes_accessed=8 * 2**20, transcendentals=0
        ),
    )(row_counts, domain_ids, domain_weights, gradients.reshape(matrices * height, width))
    full_rows = height * shards
    updates = finished.reshape(mats, height, width).astype(F32) * (
        MUON_SCALE * math.sqrt(full_rows)
    )
    return (updates, new_weights[0, :groups])


def solution(mesh):
    placed = (P("domain", None, "fsdp", None), P(), P(), P())
    return jax.shard_map(
        body,
        mesh=mesh,
        in_specs=placed,
        out_specs=(P("domain", "fsdp", None), P()),
        check_vma=False,
    )
```

```python
import functools
import math

import jax
import jax.numpy as jnp
from jax import lax
from jax.experimental import pallas as pl
from jax.experimental.pallas import tpu as pltpu
from jax.sharding import PartitionSpec as P

COEF_A = 3.4445
COEF_B = -4.775
COEF_C = 2.0315
MUON_SCALE = 0.2
ETA = 4.0
F32 = jnp.float32
BF16 = jnp.bfloat16
CORES = 2
RING = 4


def kernel(
    sizes,
    counts_ref, ids_ref, weights_ref, grads_ref,
    out_ref, new_ref,
    own, sib, far_out, near_out, far_in, near_in, comb, rows, done, relay,
    gram, gram_in, term, lin0, lin1, gram_b, term_b, lin0_b, lin1_b, score, sq_acc,
    own_sem, sib_send, sib_recv, far_send, far_recv, near_send, near_recv,
    ag_send, ag_recv, in_send, in_recv, out_send, out_recv,
    relay_recv, pass_send, red_send, red_recv, swap_send, swap_recv, known,
):
    groups, y_size, z_size, z_low, mats, height, width = sizes
    z_high = z_size // z_low
    bands = z_size // CORES
    pair = mats // 4
    d = lax.axis_index("domain")
    f = lax.axis_index("fsdp")
    x, core = d // CORES, d % CORES
    y, z = f // z_size, f % z_size
    zh, zl = z // z_low, z % z_low
    sibling = CORES * x + (1 - core)
    ring = [(x + step) % RING for step in (2, 1, 3, 0)]
    plus, minus = CORES * ring[1] + core, CORES * ring[2] + core
    own_slot, holder = z % mats, z // mats
    is_owner = y == z % y_size
    role = jnp.where(core == holder, 0, 1)
    owned_block = CORES * x + holder
    skew = (y + y_size - z % y_size) % y_size

    def owner(j):
        return j % y_size * z_size + j + mats * core

    def remote(src, dst, send, recv, dd, ff):
        return pltpu.make_async_remote_copy(
            src_ref=src, dst_ref=dst, send_sem=send, recv_sem=recv,
            device_id=(dd, ff), device_id_type=pl.DeviceIdType.MESH,
        )

    def block(ref, first, count=1):
        return ref.at[pl.ds(first * height, count * height)]

    barrier = pltpu.get_barrier_semaphore()

    def greet(dd, ff):
        pl.semaphore_signal(
            barrier, inc=1, device_id=(dd, ff), device_id_type=pl.DeviceIdType.MESH
        )

    half = mats // 2

    def own_copy(rel, stage):
        first = mats * (CORES * ring[rel] + core) + half * stage
        return pltpu.make_async_copy(
            block(grads_ref, first, half),
            block(own, rel * mats + half * stage, half),
            own_sem.at[rel, stage],
        )

    def sib_copy(rel, stage):
        first = mats * (CORES * ring[rel] + (1 - core)) + half * stage
        return remote(
            block(grads_ref, first, half),
            block(sib, rel * mats + half * stage, half),
            sib_send.at[rel, stage], sib_recv.at[rel, stage], sibling, f,
        )

    order = [(0, 0), (1, 0), (2, 0), (3, 0), (0, 1), (1, 1), (2, 1), (3, 1)]
    for rel, stage in order:
        own_copy(rel, stage).start()

    def at_y(step):
        return d, (y + step) % y_size * z_size + z

    def at_low(step):
        return d, y * z_size + zh * z_low + (zl + step) % z_low

    def at_high(step):
        return d, y * z_size + (zh + step) % z_high * z_low + zl

    def at_x(step):
        return CORES * ((x + step) % RING) + core, f

    greet(sibling, f)
    for size, where in ((RING, at_x), (y_size, at_y), (z_low, at_low), (z_high, at_high)):
        for step in range(1, size):
            greet(*where(step))
    pl.semaphore_wait(barrier, 1 + (RING - 1) + (y_size - 1) + (z_low - 1) + (z_high - 1))

    relays = ((z_high, at_high), (y_size, at_y), (2, lambda step: (sibling, f)))

    def tell(stage):
        size, where = relays[stage]
        for step in range(1, size):
            dd, ff = where(step)
            pl.semaphore_signal(
                known.at[stage], inc=1, device_id=(dd, ff),
                device_id_type=pl.DeviceIdType.MESH,
            )

    def hear(stage):
        pl.semaphore_wait(known.at[stage], relays[stage][0] - 1)

    tell(0)
    for rel, stage in order:
        sib_copy(rel, stage).start()

    total_weight = weights_ref[0]
    for k in range(1, groups):
        total_weight = total_weight + weights_ref[k]

    def mix_row(group):
        kind = ids_ref[group]
        count = jnp.float32(0)
        for h in range(groups):
            count = count + jnp.where(ids_ref[h] == kind, 1.0, 0.0)
        full = lambda value: jnp.full((1, width), value, F32)
        return full(weights_ref[kind]) / full(total_weight) / jnp.maximum(full(count), 1.0)

    mix_own, mix_sib = mix_row(d), mix_row(sibling)

    def keep(rel, j):
        index = mats * (CORES * ring[rel] + core) + j
        return jnp.where(f * height < counts_ref[index], 1.0, 0.0)

    def partial(rel, j):
        at = pl.ds((rel * mats + j) * height, height)
        kept = keep(rel, j)
        return (mix_own * kept) * own[at, :].astype(F32) + (mix_sib * kept) * sib[
            at, :
        ].astype(F32)

    def arrived(rel, stage):
        own_copy(rel, stage).wait()
        sib_copy(rel, stage).wait_recv()

    def far_copy(way, stage):
        part = way * 2 + stage
        return remote(
            block(far_out, part * pair, pair), block(far_in, part * pair, pair),
            far_send.at[part], far_recv.at[part], (plus, minus)[way], f,
        )

    def near_copy(way, quarter):
        first = way * mats + quarter * pair
        return remote(
            block(near_out, first, pair), block(near_in, first, pair),
            near_send.at[way, quarter], near_recv.at[way, quarter], (plus, minus)[way], f,
        )

    def send_far(stage):
        arrived(0, stage)
        for way in (0, 1):
            for i in range(pair):
                at = pl.ds(((way * 2 + stage) * pair + i) * height, height)
                far_out[at, :] = partial(0, (2 * stage + way) * pair + i).astype(BF16)
            far_copy(way, stage).start()

    def send_near(stage):
        for way in (0, 1):
            arrived(1 + way, stage)
            quarter = 2 * stage + 1 - way
            for i in range(pair):
                j = quarter * pair + i
                at = pl.ds((way * mats + j) * height, height)
                near_out[at, :] = partial(1 + way, j).astype(BF16)
            near_copy(way, quarter).start()

    def send_merged(stage):
        for way in (0, 1):
            far_copy(way, stage).wait_recv()
            quarter = 2 * stage + way
            for i in range(pair):
                j = quarter * pair + i
                at = pl.ds((way * mats + j) * height, height)
                came = pl.ds(((way * 2 + stage) * pair + i) * height, height)
                near_out[at, :] = (
                    partial(1 + way, j) + far_in[came, :].astype(F32)
                ).astype(BF16)
            near_copy(way, quarter).start()

    odd = z % CORES
    slot_here = z // CORES * y_size + y

    def in_copy(j):
        return remote(
            block(comb, 3 * mats + j), block(rows, slot_here),
            in_send.at[j], in_recv.at[z // CORES],
            jnp.where(odd == 0, d, sibling), owner(j),
        )

    def stays(j):
        return jnp.logical_and(f == owner(j), odd == 0)

    def combine(stage):
        arrived(3, stage)
        for quarter in (2 * stage, 2 * stage + 1):
            for way in (0, 1):
                near_copy(way, quarter).wait_recv()
            for i in range(pair):
                j = quarter * pair + i
                left = pl.ds(j * height, height)
                right = pl.ds((mats + j) * height, height)
                value = partial(3, j) + (
                    near_in[left, :].astype(F32) + near_in[right, :].astype(F32)
                )
                sq_acc[...] += jnp.sum(
                    (value * value).reshape(height // 8, 8, width), axis=0
                )
                comb[pl.ds((3 * mats + j) * height, height), :] = value.astype(BF16)
        for i in range(half):
            j = half * stage + (i + z + y) % half

            @pl.when(jnp.logical_not(stays(j)))
            def _():
                in_copy(j).start()

            @pl.when(stays(j))
            def _():
                pltpu.make_async_copy(
                    block(comb, 3 * mats + j), block(rows, slot_here),
                    in_recv.at[z // CORES],
                ).start()

    def ag_copy(step, stage):
        first = half * stage
        return remote(
            block(comb, 3 * mats + first, half),
            block(comb, (3, 2, 0, 1)[step] * mats + first, half),
            ag_send.at[step, stage], ag_recv.at[step, stage], *at_x(step),
        )

    def gather(stage):
        for step in range(1, RING):
            ag_copy(step, stage).start()

    sq_acc[...] = jnp.zeros_like(sq_acc)
    send_far(0)
    hear(0)
    tell(1)
    send_near(0)
    hear(1)
    tell(2)
    send_merged(0)
    send_far(1)
    hear(2)
    combine(0)
    send_near(1)
    send_merged(1)
    combine(1)
    gather(0)
    gather(1)

    band = y_size * height

    def near_band(step):
        shift = jnp.where(step % 2 == 1, (step + 1) // 2, bands - step // 2)
        return (z // CORES + shift) % bands

    swap = remote(gram, gram_in, swap_send, swap_recv, sibling, f)

    @pl.when(is_owner)
    def _():
        gram[...] = jnp.zeros_like(gram)

        def one(step, carry):
            index = near_band(step)
            here = rows.at[pl.ds(index * band, band)]
            pltpu.make_async_copy(here, here, in_recv.at[index]).wait()
            part = here[...]
            gram[...] += lax.dot_general(
                part, part, (((0,), (0,)), ((), ())), preferred_element_type=F32
            )
            return carry

        lax.fori_loop(0, bands, one, 0)
        swap.start()

    for stage in (0, 1):
        for step in range(1, RING):
            ag_copy(step, stage).wait_recv()

    fold = lambda value: jnp.sum(value.reshape(height // 8, 8, width), axis=0)

    def align(index, carry):
        rel, j = index // mats, index % mats
        step = jnp.where(rel == 0, 2, jnp.where(rel == 1, 1, jnp.where(rel == 2, 3, 0)))
        matrix = mats * (CORES * ((x + step) % RING) + core) + j
        kept = jnp.where(f * height < counts_ref[matrix], 1.0, 0.0)
        at = pl.ds(index * height, height)
        mine, other = own[at, :].astype(F32), sib[at, :].astype(F32)
        both = comb[at, :].astype(F32)
        return (
            carry[0] + fold(mine * both),
            carry[1] + fold(other * both),
            carry[2] + kept * fold(mine * mine),
            carry[3] + kept * fold(other * other),
        )

    empty = jnp.zeros((8, width), F32)
    sums = lax.fori_loop(0, RING * mats, align, (empty,) * 4)
    sums = [
        jnp.sum(jnp.sum(value, axis=0, keepdims=True), axis=1, keepdims=True)
        for value in (*sums, sq_acc[...])
    ]
    sub = lax.broadcasted_iota(jnp.int32, (8, 128), 0)
    lane = lax.broadcasted_iota(jnp.int32, (8, 128), 1)

    def by_group(mine, other):
        return jnp.where(sub == d, mine, jnp.where(sub == sibling, other, 0.0))

    tile = jnp.where(
        lane == 0,
        by_group(sums[0], sums[1]),
        jnp.where(
            lane == 1,
            by_group(sums[2], sums[3]),
            jnp.where(lane == 2, sums[4], 0.0),
        ),
    )
    def at_skew(z_to):
        return d, (z_to + skew) % y_size * z_size + z_to

    stages = (
        (y_size, y, at_y),
        (z_low, zl, lambda step: at_skew(zh * z_low + (zl + step) % z_low)),
        (z_high, zh, lambda step: at_skew((zh + step) % z_high * z_low + zl)),
        (CORES, core, lambda step: (sibling, f)),
        (RING, x, at_x),
    )
    bases = [sum(size for size, _, _ in stages[:stage]) for stage in range(6)]
    last = bases[5]

    def red_copy(stage, step):
        size, place, where = stages[stage]
        mine = score.at[bases[stage] + place]
        return remote(
            mine, mine, red_send.at[bases[stage] + step],
            red_recv.at[bases[stage] + place], *where(step),
        )

    def to_owner(step):
        return (y + step) % y_size == z % y_size

    def last_copy():
        return remote(
            score.at[last], score.at[last], red_send.at[last], red_recv.at[last],
            d, z % y_size * z_size + z,
        )

    def hand_in(stage, value):
        size, place, _ = stages[stage]
        score[bases[stage] + place] = value
        for step in range(1, size):
            if stage == 0:

                @pl.when(jnp.logical_not(to_owner(step)))
                def _():
                    red_copy(stage, step).start()

            else:
                red_copy(stage, step).start()

    def summed(stage):
        size, place, _ = stages[stage]
        for step in range(1, size):
            slot = bases[stage] + (place + step) % size
            pltpu.make_async_copy(score.at[slot], score.at[slot], red_recv.at[slot]).wait()
        value = score[bases[stage]]
        for i in range(1, size):
            value = value + score[bases[stage] + i]
        return value

    hand_in(0, tile)

    def out_place(index, y_to):
        return y_to * z_size + CORES * index + role

    def out_stays(index, y_to):
        return jnp.logical_and(role == 0, out_place(index, y_to) == f)

    def relay_copy(index, y_to):
        slot = index * y_size + y_to
        return remote(
            block(done, slot), block(relay, index),
            out_send.at[slot], relay_recv.at[index], d, y_to * z_size + z,
        )

    def out_copy(index, y_to):
        slot = index * y_size + y_to
        return remote(
            block(done, slot), block(out_ref, own_slot),
            out_send.at[slot], out_recv.at[own_slot],
            owned_block, out_place(index, y_to),
        )

    @pl.when(is_owner)
    def _():
        row_id = lax.broadcasted_iota(jnp.int32, (width, width), 0)
        col_id = lax.broadcasted_iota(jnp.int32, (width, width), 1)
        swap.wait_recv()
        gram_in[...] += gram[...]
        swap.wait_send()
        trace = jnp.sum(
            jnp.where(row_id == col_id, gram_in[...], 0.0), axis=0, keepdims=True
        )
        trace = jnp.sum(trace, axis=1, keepdims=True)
        scale = 1.0 / (jnp.sqrt(trace) + 1e-07)
        dot = lambda a, b: jnp.dot(a[...], b[...], preferred_element_type=F32)

        gram[...] = gram_in[...] * scale * scale
        gram_b[...] = gram[...].astype(BF16)
        for lin, lin_b in ((lin0, lin0_b), (lin1, lin1_b)):
            lin[...] = COEF_B * gram[...] + COEF_C * dot(gram_b, gram_b)
            lin_b[...] = lin[...].astype(BF16)
            term[...] = COEF_A * gram[...] + dot(lin_b, gram_b)
            term_b[...] = term[...].astype(BF16)
            gram[...] = COEF_A * term[...] + dot(lin_b, term_b)
            gram_b[...] = gram[...].astype(BF16)
        lin0[...] = COEF_A * (lin0[...] + lin1[...]) + dot(lin0_b, lin1_b)
        lin0_b[...] = lin0[...].astype(BF16)
        lin1[...] = COEF_B * gram[...] + COEF_C * dot(gram_b, gram_b)
        lin1_b[...] = lin1[...].astype(BF16)
        whole = COEF_A**2 * lin1[...] + COEF_A * lin0[...] + dot(lin0_b, lin1_b)
        whole = whole + jnp.where(row_id == col_id, COEF_A**3, 0.0)
        gram_b[...] = (whole * scale).astype(BF16)

        def one(step, carry):
            index = near_band(bands - 1 - step)
            at = pl.ds(index * band, band)
            done[at, :] = jnp.dot(
                rows[at, :], gram_b[...], preferred_element_type=F32
            ).astype(BF16)
            for y_to in range(y_size):
                here = out_stays(index, y_to)

                @pl.when(y_to != y)
                def _():
                    relay_copy(index, y_to).start()

                @pl.when(jnp.logical_and(y_to == y, jnp.logical_not(here)))
                def _():
                    out_copy(index, y_to).start()

                @pl.when(here)
                def _():
                    pltpu.make_async_copy(
                        block(done, index * y_size + y_to), block(out_ref, own_slot),
                        out_recv.at[own_slot],
                    ).start()

            return carry

        lax.fori_loop(0, bands, one, 0)

    def pass_copy(index):
        return remote(
            block(relay, index), block(out_ref, own_slot),
            pass_send.at[index], out_recv.at[own_slot],
            owned_block, out_place(index, y),
        )

    @pl.when(jnp.logical_not(is_owner))
    def _():
        step = 0
        for stage in range(5):
            value = summed(stage)
            if stage == 4:
                score[last] = value
                break
            hand_in(stage + 1, value)
            for _ in range(bands // 4):
                index = near_band(bands - 1 - step)
                step += 1
                here = block(relay, index)
                pltpu.make_async_copy(here, here, relay_recv.at[index]).wait()
                stay = out_stays(index, y)

                @pl.when(jnp.logical_not(stay))
                def _():
                    pass_copy(index).start()

                @pl.when(stay)
                def _():
                    pltpu.make_async_copy(
                        block(relay, index), block(out_ref, own_slot),
                        out_recv.at[own_slot],
                    ).start()

    @pl.when(skew == 1)
    def _():
        last_copy().start()

    @pl.when(is_owner)
    def _():
        last_copy().wait_recv()

    tile = score[last]
    id_col = jnp.zeros((8, 128), jnp.int32)
    weight_row = jnp.zeros((1, 128), F32)
    for g in range(groups):
        id_col = jnp.where(sub == g, ids_ref[g], id_col)
        weight_row = jnp.where(lane[:1] == g, weights_ref[g], weight_row)
    column = lambda k: jnp.sum(jnp.where(lane == k, tile, 0.0), axis=1, keepdims=True)
    aligned, squares, total_sq = column(0), column(1), column(2)
    cosine = aligned / (jnp.sqrt(squares) * jnp.sqrt(total_sq) + 1e-06)
    onehot = jnp.where(id_col == lane, 1.0, 0.0)
    kind_counts = jnp.sum(onehot, axis=0, keepdims=True)
    points = jnp.sum(onehot * cosine, axis=0, keepdims=True) / jnp.maximum(kind_counts, 1.0)
    share = weight_row / jnp.full((1, 128), total_weight, F32)
    raised = share * jnp.exp(ETA * points)
    new_ref[...] = raised / jnp.sum(raised, axis=1, keepdims=True)

    for rel, stage in order:
        sib_copy(rel, stage).wait_send()
    for way in (0, 1):
        for stage in (0, 1):
            far_copy(way, stage).wait_send()
        for quarter in range(4):
            near_copy(way, quarter).wait_send()
    for stage in (0, 1):
        for step in range(1, RING):
            ag_copy(step, stage).wait_send()
    for j in range(mats):

        @pl.when(jnp.logical_not(stays(j)))
        def _():
            in_copy(j).wait_send()

    for step in range(1, y_size):

        @pl.when(jnp.logical_not(to_owner(step)))
        def _():
            red_copy(0, step).wait_send()

    @pl.when(skew == 1)
    def _():
        last_copy().wait_send()

    @pl.when(is_owner)
    def _():
        def one(index, carry):
            for y_to in range(y_size):

                @pl.when(jnp.logical_not(out_stays(index, y_to)))
                def _():
                    out_copy(index, y_to).wait_send()

            return carry

        lax.fori_loop(0, bands, one, 0)

    @pl.when(jnp.logical_not(is_owner))
    def _():
        for stage in range(1, 5):
            for step in range(1, stages[stage][0]):
                red_copy(stage, step).wait_send()

        def one(index, carry):

            @pl.when(jnp.logical_not(out_stays(index, y)))
            def _():
                pass_copy(index).wait_send()

            return carry

        lax.fori_loop(0, bands, one, 0)

    for j in range(mats):
        here = block(out_ref, j)
        pltpu.make_async_copy(here, here, out_recv.at[j]).wait()


def body(gradients, row_counts, domain_ids, domain_weights):
    groups = lax.axis_size("domain")
    shards = lax.axis_size("fsdp")
    matrices, height, width = gradients.shape[1:]
    mats = matrices // groups
    y_size = 4 if shards == 64 else 2
    z_size = shards // y_size
    z_low = 4 if z_size == 16 else 2
    sizes = (groups, y_size, z_size, z_low, mats, height, width)
    assert groups == CORES * RING
    block = lambda count: pltpu.VMEM((count * height, width), BF16)
    square = lambda dtype: pltpu.VMEM((width, width), dtype)
    dma = lambda *shape: pltpu.SemaphoreType.DMA(shape)
    red = CORES + RING + y_size + z_low + z_size // z_low + 1
    assert z_size == CORES * mats and mats % y_size == 0
    held = shards // CORES
    finished, new_weights = pl.pallas_call(
        functools.partial(kernel, sizes),
        out_shape=(
            jax.ShapeDtypeStruct((mats * height, width), BF16),
            jax.ShapeDtypeStruct((1, 128), F32),
        ),
        in_specs=[pl.BlockSpec(memory_space=pltpu.SMEM)] * 3
        + [pl.BlockSpec(memory_space=pl.ANY)],
        out_specs=(
            pl.BlockSpec(memory_space=pl.ANY),
            pl.BlockSpec(memory_space=pltpu.VMEM),
        ),
        scratch_shapes=[
            block(RING * mats), block(RING * mats), block(mats), block(2 * mats),
            block(mats), block(2 * mats), block(RING * mats), block(held), block(held), block(z_size // CORES),
            *[square(F32)] * 5,
            *[square(BF16)] * 4,
            pltpu.VMEM((red, 8, 128), F32), pltpu.VMEM((8, width), F32),
            dma(4, 2), dma(4, 2), dma(4, 2), dma(4), dma(4), dma(2, 4), dma(2, 4),
            dma(4, 2), dma(4, 2), dma(mats), dma(z_size // CORES),
            dma(held), dma(mats), dma(z_size // CORES), dma(z_size // CORES), dma(red), dma(red), pltpu.SemaphoreType.DMA,
            pltpu.SemaphoreType.DMA, pltpu.SemaphoreType.REGULAR((3,)),
        ],
        compiler_params=pltpu.CompilerParams(
            collective_id=0, has_side_effects=True, vmem_limit_bytes=60 * 2**20
        ),
        cost_estimate=pl.CostEstimate(
            flops=20 * 10**9, bytes_accessed=8 * 2**20, transcendentals=0
        ),
    )(row_counts, domain_ids, domain_weights, gradients.reshape(matrices * height, width))
    full_rows = height * shards
    updates = finished.reshape(mats, height, width).astype(F32) * (
        MUON_SCALE * math.sqrt(full_rows)
    )
    return (updates, new_weights[0, :groups])


def solution(mesh):
    placed = (P("domain", None, "fsdp", None), P(), P(), P())
    return jax.shard_map(
        body,
        mesh=mesh,
        in_specs=placed,
        out_specs=(P("domain", "fsdp", None), P()),
        check_vma=False,
    )
```

```python
import functools
import math

import jax
import jax.numpy as jnp
from jax import lax
from jax.experimental import pallas as pl
from jax.experimental.pallas import tpu as pltpu
from jax.sharding import PartitionSpec as P

COEF_A = 3.4445
COEF_B = -4.775
COEF_C = 2.0315
MUON_SCALE = 0.2
ETA = 4.0
F32 = jnp.float32
BF16 = jnp.bfloat16
CORES = 2
RING = 4


def kernel(
    sizes,
    counts_ref, ids_ref, weights_ref, grads_ref,
    out_ref, new_ref,
    own, sib, far_out, near_out, far_in, near_in, comb, rows, done, relay,
    gram, gram_in, term, lin0, lin1, gram_b, term_b, lin0_b, lin1_b, score, sq_acc,
    own_sem, sib_send, sib_recv, far_send, far_recv, near_send, near_recv,
    ag_send, ag_recv, in_send, in_recv, out_send, out_recv,
    relay_recv, pass_send, red_send, red_recv, swap_send, swap_recv, known,
):
    groups, y_size, z_size, z_low, mats, height, width = sizes
    z_high = z_size // z_low
    bands = z_size // CORES
    pair = mats // 4
    d = lax.axis_index("domain")
    f = lax.axis_index("fsdp")
    x, core = d // CORES, d % CORES
    y, z = f // z_size, f % z_size
    zh, zl = z // z_low, z % z_low
    sibling = CORES * x + (1 - core)
    ring = [(x + step) % RING for step in (2, 1, 3, 0)]
    plus, minus = CORES * ring[1] + core, CORES * ring[2] + core
    own_slot, holder = z % mats, z // mats
    is_owner = y == z % y_size
    role = jnp.where(core == holder, 0, 1)
    owned_block = CORES * x + holder
    skew = (y + y_size - z % y_size) % y_size

    def owner(j):
        return j % y_size * z_size + j + mats * core

    def remote(src, dst, send, recv, dd, ff):
        return pltpu.make_async_remote_copy(
            src_ref=src, dst_ref=dst, send_sem=send, recv_sem=recv,
            device_id=(dd, ff), device_id_type=pl.DeviceIdType.MESH,
        )

    def block(ref, first, count=1):
        return ref.at[pl.ds(first * height, count * height)]

    barrier = pltpu.get_barrier_semaphore()

    def greet(dd, ff):
        pl.semaphore_signal(
            barrier, inc=1, device_id=(dd, ff), device_id_type=pl.DeviceIdType.MESH
        )

    half = mats // 2

    def own_copy(rel, stage):
        first = mats * (CORES * ring[rel] + core) + half * stage
        return pltpu.make_async_copy(
            block(grads_ref, first, half),
            block(own, rel * mats + half * stage, half),
            own_sem.at[rel, stage],
        )

    def sib_copy(rel, stage):
        first = mats * (CORES * ring[rel] + (1 - core)) + half * stage
        return remote(
            block(grads_ref, first, half),
            block(sib, rel * mats + half * stage, half),
            sib_send.at[rel, stage], sib_recv.at[rel, stage], sibling, f,
        )

    order = [(0, 0), (1, 0), (2, 0), (3, 0), (0, 1), (1, 1), (2, 1), (3, 1)]
    for rel, stage in order:
        own_copy(rel, stage).start()

    def at_y(step):
        return d, (y + step) % y_size * z_size + z

    def at_low(step):
        return d, y * z_size + zh * z_low + (zl + step) % z_low

    def at_high(step):
        return d, y * z_size + (zh + step) % z_high * z_low + zl

    def at_x(step):
        return CORES * ((x + step) % RING) + core, f

    greet(sibling, f)
    for size, where in ((RING, at_x), (y_size, at_y), (z_low, at_low), (z_high, at_high)):
        for step in range(1, size):
            greet(*where(step))
    pl.semaphore_wait(barrier, 1 + (RING - 1) + (y_size - 1) + (z_low - 1) + (z_high - 1))

    relays = ((z_high, at_high), (y_size, at_y), (2, lambda step: (sibling, f)))

    def tell(stage):
        size, where = relays[stage]
        for step in range(1, size):
            dd, ff = where(step)
            pl.semaphore_signal(
                known.at[stage], inc=1, device_id=(dd, ff),
                device_id_type=pl.DeviceIdType.MESH,
            )

    def hear(stage):
        pl.semaphore_wait(known.at[stage], relays[stage][0] - 1)

    tell(0)
    for rel, stage in order:
        sib_copy(rel, stage).start()

    total_weight = weights_ref[0]
    for k in range(1, groups):
        total_weight = total_weight + weights_ref[k]

    def mix_row(group):
        kind = ids_ref[group]
        count = jnp.float32(0)
        for h in range(groups):
            count = count + jnp.where(ids_ref[h] == kind, 1.0, 0.0)
        full = lambda value: jnp.full((1, width), value, F32)
        return full(weights_ref[kind]) / full(total_weight) / jnp.maximum(full(count), 1.0)

    mix_own, mix_sib = mix_row(d), mix_row(sibling)

    def keep(rel, j):
        index = mats * (CORES * ring[rel] + core) + j
        return jnp.where(f * height < counts_ref[index], 1.0, 0.0)

    def partial(rel, j):
        at = pl.ds((rel * mats + j) * height, height)
        kept = keep(rel, j)
        return (mix_own * kept) * own[at, :].astype(F32) + (mix_sib * kept) * sib[
            at, :
        ].astype(F32)

    def arrived(rel, stage):
        own_copy(rel, stage).wait()
        sib_copy(rel, stage).wait_recv()

    def far_copy(way, stage):
        part = way * 2 + stage
        return remote(
            block(far_out, part * pair, pair), block(far_in, part * pair, pair),
            far_send.at[part], far_recv.at[part], (plus, minus)[way], f,
        )

    def near_copy(way, quarter):
        first = way * mats + quarter * pair
        return remote(
            block(near_out, first, pair), block(near_in, first, pair),
            near_send.at[way, quarter], near_recv.at[way, quarter], (plus, minus)[way], f,
        )

    def send_far(stage):
        arrived(0, stage)
        for way in (0, 1):
            for i in range(pair):
                at = pl.ds(((way * 2 + stage) * pair + i) * height, height)
                far_out[at, :] = partial(0, (2 * stage + way) * pair + i).astype(BF16)
            far_copy(way, stage).start()

    def send_near(stage):
        for way in (0, 1):
            arrived(1 + way, stage)
            quarter = 2 * stage + 1 - way
            for i in range(pair):
                j = quarter * pair + i
                at = pl.ds((way * mats + j) * height, height)
                near_out[at, :] = partial(1 + way, j).astype(BF16)
            near_copy(way, quarter).start()

    def send_merged(stage):
        for way in (0, 1):
            far_copy(way, stage).wait_recv()
            quarter = 2 * stage + way
            for i in range(pair):
                j = quarter * pair + i
                at = pl.ds((way * mats + j) * height, height)
                came = pl.ds(((way * 2 + stage) * pair + i) * height, height)
                near_out[at, :] = (
                    partial(1 + way, j) + far_in[came, :].astype(F32)
                ).astype(BF16)
            near_copy(way, quarter).start()

    odd = z % CORES
    slot_here = z // CORES * y_size + y

    def in_copy(j):
        return remote(
            block(comb, 3 * mats + j), block(rows, slot_here),
            in_send.at[j], in_recv.at[z // CORES],
            jnp.where(odd == 0, d, sibling), owner(j),
        )

    def stays(j):
        return jnp.logical_and(f == owner(j), odd == 0)

    def combine(stage):
        arrived(3, stage)
        for quarter in (2 * stage, 2 * stage + 1):
            for way in (0, 1):
                near_copy(way, quarter).wait_recv()
            for i in range(pair):
                j = quarter * pair + i
                left = pl.ds(j * height, height)
                right = pl.ds((mats + j) * height, height)
                value = partial(3, j) + (
                    near_in[left, :].astype(F32) + near_in[right, :].astype(F32)
                )
                sq_acc[...] += jnp.sum(
                    (value * value).reshape(height // 8, 8, width), axis=0
                )
                comb[pl.ds((3 * mats + j) * height, height), :] = value.astype(BF16)
        for i in range(half):
            j = half * stage + (i + z + y) % half

            @pl.when(jnp.logical_not(stays(j)))
            def _():
                in_copy(j).start()

            @pl.when(stays(j))
            def _():
                pltpu.make_async_copy(
                    block(comb, 3 * mats + j), block(rows, slot_here),
                    in_recv.at[z // CORES],
                ).start()

    def ag_copy(step, stage):
        first = half * stage
        return remote(
            block(comb, 3 * mats + first, half),
            block(comb, (3, 2, 0, 1)[step] * mats + first, half),
            ag_send.at[step, stage], ag_recv.at[step, stage], *at_x(step),
        )

    def gather(stage):
        for step in range(1, RING):
            ag_copy(step, stage).start()

    sq_acc[...] = jnp.zeros_like(sq_acc)
    send_far(0)
    hear(0)
    tell(1)
    send_near(0)
    hear(1)
    tell(2)
    send_merged(0)
    send_far(1)
    hear(2)
    combine(0)
    send_near(1)
    send_merged(1)
    combine(1)
    gather(0)
    gather(1)

    band = y_size * height

    def near_band(step):
        shift = jnp.where(step % 2 == 1, (step + 1) // 2, bands - step // 2)
        return (z // CORES + shift) % bands

    swap = remote(gram, gram_in, swap_send, swap_recv, sibling, f)

    def form_gram():
        gram[...] = jnp.zeros_like(gram)

        def one(step, carry):
            index = near_band(step)
            here = rows.at[pl.ds(index * band, band)]
            pltpu.make_async_copy(here, here, in_recv.at[index]).wait()
            part = here[...]
            gram[...] += lax.dot_general(
                part, part, (((0,), (0,)), ((), ())), preferred_element_type=F32
            )
            return carry

        lax.fori_loop(0, bands, one, 0)
        swap.start()

    early = own_slot < half
    pl.when(jnp.logical_and(is_owner, early))(form_gram)

    for stage in (0, 1):
        for step in range(1, RING):
            ag_copy(step, stage).wait_recv()

    fold = lambda value: jnp.sum(value.reshape(height // 8, 8, width), axis=0)

    def align(index, carry):
        rel, j = index // mats, index % mats
        step = jnp.where(rel == 0, 2, jnp.where(rel == 1, 1, jnp.where(rel == 2, 3, 0)))
        matrix = mats * (CORES * ((x + step) % RING) + core) + j
        kept = jnp.where(f * height < counts_ref[matrix], 1.0, 0.0)
        at = pl.ds(index * height, height)
        mine, other = own[at, :].astype(F32), sib[at, :].astype(F32)
        both = comb[at, :].astype(F32)
        return (
            carry[0] + fold(mine * both),
            carry[1] + fold(other * both),
            carry[2] + kept * fold(mine * mine),
            carry[3] + kept * fold(other * other),
        )

    empty = jnp.zeros((8, width), F32)
    sums = lax.fori_loop(0, RING * mats, align, (empty,) * 4)
    sums = [
        jnp.sum(jnp.sum(value, axis=0, keepdims=True), axis=1, keepdims=True)
        for value in (*sums, sq_acc[...])
    ]
    sub = lax.broadcasted_iota(jnp.int32, (8, 128), 0)
    lane = lax.broadcasted_iota(jnp.int32, (8, 128), 1)

    def by_group(mine, other):
        return jnp.where(sub == d, mine, jnp.where(sub == sibling, other, 0.0))

    tile = jnp.where(
        lane == 0,
        by_group(sums[0], sums[1]),
        jnp.where(
            lane == 1,
            by_group(sums[2], sums[3]),
            jnp.where(lane == 2, sums[4], 0.0),
        ),
    )
    def at_skew(z_to):
        return d, (z_to + skew) % y_size * z_size + z_to

    stages = (
        (y_size, y, at_y),
        (z_low, zl, lambda step: at_skew(zh * z_low + (zl + step) % z_low)),
        (z_high, zh, lambda step: at_skew((zh + step) % z_high * z_low + zl)),
        (CORES, core, lambda step: (sibling, f)),
        (RING, x, at_x),
    )
    bases = [sum(size for size, _, _ in stages[:stage]) for stage in range(6)]
    last = bases[5]

    def red_copy(stage, step):
        size, place, where = stages[stage]
        mine = score.at[bases[stage] + place]
        return remote(
            mine, mine, red_send.at[bases[stage] + step],
            red_recv.at[bases[stage] + place], *where(step),
        )

    def to_owner(step):
        return (y + step) % y_size == z % y_size

    def last_copy():
        return remote(
            score.at[last], score.at[last], red_send.at[last], red_recv.at[last],
            d, z % y_size * z_size + z,
        )

    def hand_in(stage, value):
        size, place, _ = stages[stage]
        score[bases[stage] + place] = value
        for step in range(1, size):
            if stage == 0:

                @pl.when(jnp.logical_not(to_owner(step)))
                def _():
                    red_copy(stage, step).start()

            else:
                red_copy(stage, step).start()

    def summed(stage):
        size, place, _ = stages[stage]
        for step in range(1, size):
            slot = bases[stage] + (place + step) % size
            pltpu.make_async_copy(score.at[slot], score.at[slot], red_recv.at[slot]).wait()
        value = score[bases[stage]]
        for i in range(1, size):
            value = value + score[bases[stage] + i]
        return value

    hand_in(0, tile)
    pl.when(jnp.logical_and(is_owner, jnp.logical_not(early)))(form_gram)

    def out_place(index, y_to):
        return y_to * z_size + CORES * index + role

    def out_stays(index, y_to):
        return jnp.logical_and(role == 0, out_place(index, y_to) == f)

    def relay_copy(index, y_to):
        slot = index * y_size + y_to
        return remote(
            block(done, slot), block(relay, index),
            out_send.at[slot], relay_recv.at[index], d, y_to * z_size + z,
        )

    def out_copy(index, y_to):
        slot = index * y_size + y_to
        return remote(
            block(done, slot), block(out_ref, own_slot),
            out_send.at[slot], out_recv.at[own_slot],
            owned_block, out_place(index, y_to),
        )

    @pl.when(is_owner)
    def _():
        row_id = lax.broadcasted_iota(jnp.int32, (width, width), 0)
        col_id = lax.broadcasted_iota(jnp.int32, (width, width), 1)
        swap.wait_recv()
        gram_in[...] += gram[...]
        swap.wait_send()
        trace = jnp.sum(
            jnp.where(row_id == col_id, gram_in[...], 0.0), axis=0, keepdims=True
        )
        trace = jnp.sum(trace, axis=1, keepdims=True)
        scale = 1.0 / (jnp.sqrt(trace) + 1e-07)
        dot = lambda a, b: jnp.dot(a[...], b[...], preferred_element_type=F32)

        gram[...] = gram_in[...] * scale * scale
        gram_b[...] = gram[...].astype(BF16)
        for lin, lin_b in ((lin0, lin0_b), (lin1, lin1_b)):
            lin[...] = COEF_B * gram[...] + COEF_C * dot(gram_b, gram_b)
            lin_b[...] = lin[...].astype(BF16)
            term[...] = COEF_A * gram[...] + dot(lin_b, gram_b)
            term_b[...] = term[...].astype(BF16)
            gram[...] = COEF_A * term[...] + dot(lin_b, term_b)
            gram_b[...] = gram[...].astype(BF16)
        lin0[...] = COEF_A * (lin0[...] + lin1[...]) + dot(lin0_b, lin1_b)
        lin0_b[...] = lin0[...].astype(BF16)
        lin1[...] = COEF_B * gram[...] + COEF_C * dot(gram_b, gram_b)
        lin1_b[...] = lin1[...].astype(BF16)
        whole = COEF_A**2 * lin1[...] + COEF_A * lin0[...] + dot(lin0_b, lin1_b)
        whole = whole + jnp.where(row_id == col_id, COEF_A**3, 0.0)
        gram_b[...] = (whole * scale).astype(BF16)

        def one(step, carry):
            index = near_band(bands - 1 - step)
            at = pl.ds(index * band, band)
            done[at, :] = jnp.dot(
                rows[at, :], gram_b[...], preferred_element_type=F32
            ).astype(BF16)
            for y_to in range(y_size):
                here = out_stays(index, y_to)

                @pl.when(y_to != y)
                def _():
                    relay_copy(index, y_to).start()

                @pl.when(jnp.logical_and(y_to == y, jnp.logical_not(here)))
                def _():
                    out_copy(index, y_to).start()

                @pl.when(here)
                def _():
                    pltpu.make_async_copy(
                        block(done, index * y_size + y_to), block(out_ref, own_slot),
                        out_recv.at[own_slot],
                    ).start()

            return carry

        lax.fori_loop(0, bands, one, 0)

    def pass_copy(index):
        return remote(
            block(relay, index), block(out_ref, own_slot),
            pass_send.at[index], out_recv.at[own_slot],
            owned_block, out_place(index, y),
        )

    @pl.when(jnp.logical_not(is_owner))
    def _():
        def one(step, carry):
            index = near_band(bands - 1 - step)
            here = block(relay, index)
            pltpu.make_async_copy(here, here, relay_recv.at[index]).wait()
            stay = out_stays(index, y)

            @pl.when(jnp.logical_not(stay))
            def _():
                pass_copy(index).start()

            @pl.when(stay)
            def _():
                pltpu.make_async_copy(
                    block(relay, index), block(out_ref, own_slot), out_recv.at[own_slot]
                ).start()

            return carry

        for stage in (1, 2, 3):
            hand_in(stage, summed(stage - 1))
        lax.fori_loop(0, bands // 4, one, 0)
        hand_in(4, summed(3))
        lax.fori_loop(bands // 4, bands // 2, one, 0)
        score[last] = summed(4)

        @pl.when(skew == 1)
        def _():
            last_copy().start()

        lax.fori_loop(bands // 2, bands, one, 0)

    @pl.when(is_owner)
    def _():
        last_copy().wait_recv()

    tile = score[last]
    id_col = jnp.zeros((8, 128), jnp.int32)
    weight_row = jnp.zeros((1, 128), F32)
    for g in range(groups):
        id_col = jnp.where(sub == g, ids_ref[g], id_col)
        weight_row = jnp.where(lane[:1] == g, weights_ref[g], weight_row)
    column = lambda k: jnp.sum(jnp.where(lane == k, tile, 0.0), axis=1, keepdims=True)
    aligned, squares, total_sq = column(0), column(1), column(2)
    cosine = aligned / (jnp.sqrt(squares) * jnp.sqrt(total_sq) + 1e-06)
    onehot = jnp.where(id_col == lane, 1.0, 0.0)
    kind_counts = jnp.sum(onehot, axis=0, keepdims=True)
    points = jnp.sum(onehot * cosine, axis=0, keepdims=True) / jnp.maximum(kind_counts, 1.0)
    share = weight_row / jnp.full((1, 128), total_weight, F32)
    raised = share * jnp.exp(ETA * points)
    new_ref[...] = raised / jnp.sum(raised, axis=1, keepdims=True)

    for rel, stage in order:
        sib_copy(rel, stage).wait_send()
    for way in (0, 1):
        for stage in (0, 1):
            far_copy(way, stage).wait_send()
        for quarter in range(4):
            near_copy(way, quarter).wait_send()
    for stage in (0, 1):
        for step in range(1, RING):
            ag_copy(step, stage).wait_send()
    for j in range(mats):

        @pl.when(jnp.logical_not(stays(j)))
        def _():
            in_copy(j).wait_send()

    for step in range(1, y_size):

        @pl.when(jnp.logical_not(to_owner(step)))
        def _():
            red_copy(0, step).wait_send()

    @pl.when(skew == 1)
    def _():
        last_copy().wait_send()

    @pl.when(is_owner)
    def _():
        def one(index, carry):
            for y_to in range(y_size):

                @pl.when(jnp.logical_not(out_stays(index, y_to)))
                def _():
                    out_copy(index, y_to).wait_send()

            return carry

        lax.fori_loop(0, bands, one, 0)

    @pl.when(jnp.logical_not(is_owner))
    def _():
        for stage in range(1, 5):
            for step in range(1, stages[stage][0]):
                red_copy(stage, step).wait_send()

        def one(index, carry):

            @pl.when(jnp.logical_not(out_stays(index, y)))
            def _():
                pass_copy(index).wait_send()

            return carry

        lax.fori_loop(0, bands, one, 0)

    for j in range(mats):
        here = block(out_ref, j)
        pltpu.make_async_copy(here, here, out_recv.at[j]).wait()


def body(gradients, row_counts, domain_ids, domain_weights):
    groups = lax.axis_size("domain")
    shards = lax.axis_size("fsdp")
    matrices, height, width = gradients.shape[1:]
    mats = matrices // groups
    y_size = 4 if shards == 64 else 2
    z_size = shards // y_size
    z_low = 4 if z_size == 16 else 2
    sizes = (groups, y_size, z_size, z_low, mats, height, width)
    assert groups == CORES * RING
    block = lambda count: pltpu.VMEM((count * height, width), BF16)
    square = lambda dtype: pltpu.VMEM((width, width), dtype)
    dma = lambda *shape: pltpu.SemaphoreType.DMA(shape)
    red = CORES + RING + y_size + z_low + z_size // z_low + 1
    assert z_size == CORES * mats and mats % y_size == 0
    held = shards // CORES
    finished, new_weights = pl.pallas_call(
        functools.partial(kernel, sizes),
        out_shape=(
            jax.ShapeDtypeStruct((mats * height, width), BF16),
            jax.ShapeDtypeStruct((1, 128), F32),
        ),
        in_specs=[pl.BlockSpec(memory_space=pltpu.SMEM)] * 3
        + [pl.BlockSpec(memory_space=pl.ANY)],
        out_specs=(
            pl.BlockSpec(memory_space=pl.ANY),
            pl.BlockSpec(memory_space=pltpu.VMEM),
        ),
        scratch_shapes=[
            block(RING * mats), block(RING * mats), block(mats), block(2 * mats),
            block(mats), block(2 * mats), block(RING * mats), block(held), block(held), block(z_size // CORES),
            *[square(F32)] * 5,
            *[square(BF16)] * 4,
            pltpu.VMEM((red, 8, 128), F32), pltpu.VMEM((8, width), F32),
            dma(4, 2), dma(4, 2), dma(4, 2), dma(4), dma(4), dma(2, 4), dma(2, 4),
            dma(4, 2), dma(4, 2), dma(mats), dma(z_size // CORES),
            dma(held), dma(mats), dma(z_size // CORES), dma(z_size // CORES), dma(red), dma(red), pltpu.SemaphoreType.DMA,
            pltpu.SemaphoreType.DMA, pltpu.SemaphoreType.REGULAR((3,)),
        ],
        compiler_params=pltpu.CompilerParams(
            collective_id=0, has_side_effects=True, vmem_limit_bytes=60 * 2**20
        ),
        cost_estimate=pl.CostEstimate(
            flops=20 * 10**9, bytes_accessed=8 * 2**20, transcendentals=0
        ),
    )(row_counts, domain_ids, domain_weights, gradients.reshape(matrices * height, width))
    full_rows = height * shards
    updates = finished.reshape(mats, height, width).astype(F32) * (
        MUON_SCALE * math.sqrt(full_rows)
    )
    return (updates, new_weights[0, :groups])


def solution(mesh):
    placed = (P("domain", None, "fsdp", None), P(), P(), P())
    return jax.shard_map(
        body,
        mesh=mesh,
        in_specs=placed,
        out_specs=(P("domain", "fsdp", None), P()),
        check_vma=False,
    )
```

```python
import functools
import math

import jax
import jax.numpy as jnp
from jax import lax
from jax.experimental import pallas as pl
from jax.experimental.pallas import tpu as pltpu
from jax.sharding import PartitionSpec as P

COEF_A = 3.4445
COEF_B = -4.775
COEF_C = 2.0315
MUON_SCALE = 0.2
ETA = 4.0
F32 = jnp.float32
BF16 = jnp.bfloat16
CORES = 2
RING = 4


def kernel(
    sizes,
    counts_ref, ids_ref, weights_ref, grads_ref,
    out_ref, new_ref,
    own, sib, far_out, near_out, far_in, near_in, comb, rows, done, relay,
    gram, gram_in, term, lin0, lin1, gram_b, term_b, lin0_b, lin1_b, score, sq_acc,
    own_sem, sib_send, sib_recv, far_send, far_recv, near_send, near_recv,
    ag_send, ag_recv, in_send, in_recv, out_send, out_recv,
    relay_recv, pass_send, red_send, red_recv, swap_send, swap_recv, known,
):
    groups, y_size, z_size, z_low, mats, height, width = sizes
    z_high = z_size // z_low
    bands = z_size // CORES
    pair = mats // 4
    d = lax.axis_index("domain")
    f = lax.axis_index("fsdp")
    x, core = d // CORES, d % CORES
    y, z = f // z_size, f % z_size
    zh, zl = z // z_low, z % z_low
    sibling = CORES * x + (1 - core)
    ring = [(x + step) % RING for step in (2, 1, 3, 0)]
    plus, minus = CORES * ring[1] + core, CORES * ring[2] + core
    own_slot, holder = z % mats, z // mats
    is_owner = y == z % y_size
    role = jnp.where(core == holder, 0, 1)
    owned_block = CORES * x + holder
    skew = (y + y_size - z % y_size) % y_size

    def owner(j):
        return j % y_size * z_size + j + mats * core

    def remote(src, dst, send, recv, dd, ff):
        return pltpu.make_async_remote_copy(
            src_ref=src, dst_ref=dst, send_sem=send, recv_sem=recv,
            device_id=(dd, ff), device_id_type=pl.DeviceIdType.MESH,
        )

    def block(ref, first, count=1):
        return ref.at[pl.ds(first * height, count * height)]

    barrier = pltpu.get_barrier_semaphore()

    def greet(dd, ff):
        pl.semaphore_signal(
            barrier, inc=1, device_id=(dd, ff), device_id_type=pl.DeviceIdType.MESH
        )

    half = mats // 2

    def own_copy(rel, stage):
        first = mats * (CORES * ring[rel] + core) + half * stage
        return pltpu.make_async_copy(
            block(grads_ref, first, half),
            block(own, rel * mats + half * stage, half),
            own_sem.at[rel, stage],
        )

    def sib_copy(rel, stage):
        first = mats * (CORES * ring[rel] + (1 - core)) + half * stage
        return remote(
            block(grads_ref, first, half),
            block(sib, rel * mats + half * stage, half),
            sib_send.at[rel, stage], sib_recv.at[rel, stage], sibling, f,
        )

    order = [(0, 0), (1, 0), (2, 0), (3, 0), (0, 1), (1, 1), (2, 1), (3, 1)]
    for rel, stage in order:
        own_copy(rel, stage).start()

    def at_y(step):
        return d, (y + step) % y_size * z_size + z

    def at_low(step):
        return d, y * z_size + zh * z_low + (zl + step) % z_low

    def at_high(step):
        return d, y * z_size + (zh + step) % z_high * z_low + zl

    def at_x(step):
        return CORES * ((x + step) % RING) + core, f

    greet(sibling, f)
    for size, where in ((RING, at_x), (y_size, at_y), (z_low, at_low), (z_high, at_high)):
        for step in range(1, size):
            greet(*where(step))
    pl.semaphore_wait(barrier, 1 + (RING - 1) + (y_size - 1) + (z_low - 1) + (z_high - 1))

    relays = ((z_high, at_high), (y_size, at_y), (2, lambda step: (sibling, f)))

    def tell(stage):
        size, where = relays[stage]
        for step in range(1, size):
            dd, ff = where(step)
            pl.semaphore_signal(
                known.at[stage], inc=1, device_id=(dd, ff),
                device_id_type=pl.DeviceIdType.MESH,
            )

    def hear(stage):
        pl.semaphore_wait(known.at[stage], relays[stage][0] - 1)

    tell(0)
    for rel, stage in order:
        sib_copy(rel, stage).start()

    total_weight = weights_ref[0]
    for k in range(1, groups):
        total_weight = total_weight + weights_ref[k]

    def mix_row(group):
        kind = ids_ref[group]
        count = jnp.float32(0)
        for h in range(groups):
            count = count + jnp.where(ids_ref[h] == kind, 1.0, 0.0)
        full = lambda value: jnp.full((1, width), value, F32)
        return full(weights_ref[kind]) / full(total_weight) / jnp.maximum(full(count), 1.0)

    mix_own, mix_sib = mix_row(d), mix_row(sibling)

    def keep(rel, j):
        index = mats * (CORES * ring[rel] + core) + j
        return jnp.where(f * height < counts_ref[index], 1.0, 0.0)

    def partial(rel, j):
        at = pl.ds((rel * mats + j) * height, height)
        kept = keep(rel, j)
        return (mix_own * kept) * own[at, :].astype(F32) + (mix_sib * kept) * sib[
            at, :
        ].astype(F32)

    def arrived(rel, stage):
        own_copy(rel, stage).wait()
        sib_copy(rel, stage).wait_recv()

    def far_copy(way, stage):
        part = way * 2 + stage
        return remote(
            block(far_out, part * pair, pair), block(far_in, part * pair, pair),
            far_send.at[part], far_recv.at[part], (plus, minus)[way], f,
        )

    def near_copy(way, quarter):
        first = way * mats + quarter * pair
        return remote(
            block(near_out, first, pair), block(near_in, first, pair),
            near_send.at[way, quarter], near_recv.at[way, quarter], (plus, minus)[way], f,
        )

    def send_far(stage):
        arrived(0, stage)
        for way in (0, 1):
            for i in range(pair):
                at = pl.ds(((way * 2 + stage) * pair + i) * height, height)
                far_out[at, :] = partial(0, (2 * stage + way) * pair + i).astype(BF16)
            far_copy(way, stage).start()

    def send_near(stage):
        for way in (0, 1):
            arrived(1 + way, stage)
            quarter = 2 * stage + 1 - way
            for i in range(pair):
                j = quarter * pair + i
                at = pl.ds((way * mats + j) * height, height)
                near_out[at, :] = partial(1 + way, j).astype(BF16)
            near_copy(way, quarter).start()

    def send_merged(stage):
        for way in (0, 1):
            far_copy(way, stage).wait_recv()
            quarter = 2 * stage + way
            for i in range(pair):
                j = quarter * pair + i
                at = pl.ds((way * mats + j) * height, height)
                came = pl.ds(((way * 2 + stage) * pair + i) * height, height)
                near_out[at, :] = (
                    partial(1 + way, j) + far_in[came, :].astype(F32)
                ).astype(BF16)
            near_copy(way, quarter).start()

    odd = z % CORES
    slot_here = z // CORES * y_size + y

    def in_copy(j):
        return remote(
            block(comb, 3 * mats + j), block(rows, slot_here),
            in_send.at[j], in_recv.at[z // CORES],
            jnp.where(odd == 0, d, sibling), owner(j),
        )

    def stays(j):
        return jnp.logical_and(f == owner(j), odd == 0)

    def combine(stage):
        arrived(3, stage)
        for quarter in (2 * stage, 2 * stage + 1):
            for way in (0, 1):
                near_copy(way, quarter).wait_recv()
            for i in range(pair):
                j = quarter * pair + i
                left = pl.ds(j * height, height)
                right = pl.ds((mats + j) * height, height)
                value = partial(3, j) + (
                    near_in[left, :].astype(F32) + near_in[right, :].astype(F32)
                )
                sq_acc[...] += jnp.sum(
                    (value * value).reshape(height // 8, 8, width), axis=0
                )
                comb[pl.ds((3 * mats + j) * height, height), :] = value.astype(BF16)
        for i in range(half):
            j = half * stage + (i + z + y) % half

            @pl.when(jnp.logical_not(stays(j)))
            def _():
                in_copy(j).start()

            @pl.when(stays(j))
            def _():
                pltpu.make_async_copy(
                    block(comb, 3 * mats + j), block(rows, slot_here),
                    in_recv.at[z // CORES],
                ).start()

    def ag_copy(step, stage):
        first = half * stage
        return remote(
            block(comb, 3 * mats + first, half),
            block(comb, (3, 2, 0, 1)[step] * mats + first, half),
            ag_send.at[step, stage], ag_recv.at[step, stage], *at_x(step),
        )

    def gather(stage):
        for step in range(1, RING):
            ag_copy(step, stage).start()

    sq_acc[...] = jnp.zeros_like(sq_acc)
    send_far(0)
    hear(0)
    tell(1)
    send_near(0)
    hear(1)
    tell(2)
    send_merged(0)
    send_far(1)
    hear(2)
    combine(0)
    send_near(1)
    send_merged(1)
    gather(0)
    combine(1)
    gather(1)

    band = y_size * height

    def near_band(step):
        shift = jnp.where(step % 2 == 1, (step + 1) // 2, bands - step // 2)
        return (z // CORES + shift) % bands

    swap = remote(gram, gram_in, swap_send, swap_recv, sibling, f)

    def form_gram():
        gram[...] = jnp.zeros_like(gram)

        def one(step, carry):
            index = near_band(step)
            here = rows.at[pl.ds(index * band, band)]
            pltpu.make_async_copy(here, here, in_recv.at[index]).wait()
            part = here[...]
            gram[...] += lax.dot_general(
                part, part, (((0,), (0,)), ((), ())), preferred_element_type=F32
            )
            return carry

        lax.fori_loop(0, bands, one, 0)
        swap.start()

    early = own_slot < half
    pl.when(jnp.logical_and(is_owner, early))(form_gram)

    for stage in (0, 1):
        for step in range(1, RING):
            ag_copy(step, stage).wait_recv()

    fold = lambda value: jnp.sum(value.reshape(height // 8, 8, width), axis=0)

    def align(index, carry):
        rel, j = index // mats, index % mats
        step = jnp.where(rel == 0, 2, jnp.where(rel == 1, 1, jnp.where(rel == 2, 3, 0)))
        matrix = mats * (CORES * ((x + step) % RING) + core) + j
        kept = jnp.where(f * height < counts_ref[matrix], 1.0, 0.0)
        at = pl.ds(index * height, height)
        mine, other = own[at, :].astype(F32), sib[at, :].astype(F32)
        both = comb[at, :].astype(F32)
        return (
            carry[0] + fold(mine * both),
            carry[1] + fold(other * both),
            carry[2] + kept * fold(mine * mine),
            carry[3] + kept * fold(other * other),
        )

    empty = jnp.zeros((8, width), F32)
    sums = lax.fori_loop(0, RING * mats, align, (empty,) * 4)
    sums = [
        jnp.sum(jnp.sum(value, axis=0, keepdims=True), axis=1, keepdims=True)
        for value in (*sums, sq_acc[...])
    ]
    sub = lax.broadcasted_iota(jnp.int32, (8, 128), 0)
    lane = lax.broadcasted_iota(jnp.int32, (8, 128), 1)

    def by_group(mine, other):
        return jnp.where(sub == d, mine, jnp.where(sub == sibling, other, 0.0))

    tile = jnp.where(
        lane == 0,
        by_group(sums[0], sums[1]),
        jnp.where(
            lane == 1,
            by_group(sums[2], sums[3]),
            jnp.where(lane == 2, sums[4], 0.0),
        ),
    )
    def at_skew(z_to):
        return d, (z_to + skew) % y_size * z_size + z_to

    stages = (
        (y_size, y, at_y),
        (z_low, zl, lambda step: at_skew(zh * z_low + (zl + step) % z_low)),
        (z_high, zh, lambda step: at_skew((zh + step) % z_high * z_low + zl)),
        (CORES, core, lambda step: (sibling, f)),
        (RING, x, at_x),
    )
    bases = [sum(size for size, _, _ in stages[:stage]) for stage in range(6)]
    last = bases[5]

    def red_copy(stage, step):
        size, place, where = stages[stage]
        mine = score.at[bases[stage] + place]
        return remote(
            mine, mine, red_send.at[bases[stage] + step],
            red_recv.at[bases[stage] + place], *where(step),
        )

    def to_owner(step):
        return (y + step) % y_size == z % y_size

    def last_copy():
        return remote(
            score.at[last], score.at[last], red_send.at[last], red_recv.at[last],
            d, z % y_size * z_size + z,
        )

    def hand_in(stage, value):
        size, place, _ = stages[stage]
        score[bases[stage] + place] = value
        for step in range(1, size):
            if stage == 0:

                @pl.when(jnp.logical_not(to_owner(step)))
                def _():
                    red_copy(stage, step).start()

            else:
                red_copy(stage, step).start()

    def summed(stage):
        size, place, _ = stages[stage]
        for step in range(1, size):
            slot = bases[stage] + (place + step) % size
            pltpu.make_async_copy(score.at[slot], score.at[slot], red_recv.at[slot]).wait()
        value = score[bases[stage]]
        for i in range(1, size):
            value = value + score[bases[stage] + i]
        return value

    hand_in(0, tile)
    pl.when(jnp.logical_and(is_owner, jnp.logical_not(early)))(form_gram)

    def out_place(index, y_to):
        return y_to * z_size + CORES * index + role

    def out_stays(index, y_to):
        return jnp.logical_and(role == 0, out_place(index, y_to) == f)

    def relay_copy(index, y_to):
        slot = index * y_size + y_to
        return remote(
            block(done, slot), block(relay, index),
            out_send.at[slot], relay_recv.at[index], d, y_to * z_size + z,
        )

    def out_copy(index, y_to):
        slot = index * y_size + y_to
        return remote(
            block(done, slot), block(out_ref, own_slot),
            out_send.at[slot], out_recv.at[own_slot],
            owned_block, out_place(index, y_to),
        )

    @pl.when(is_owner)
    def _():
        row_id = lax.broadcasted_iota(jnp.int32, (width, width), 0)
        col_id = lax.broadcasted_iota(jnp.int32, (width, width), 1)
        swap.wait_recv()
        gram_in[...] += gram[...]
        swap.wait_send()
        trace = jnp.sum(
            jnp.where(row_id == col_id, gram_in[...], 0.0), axis=0, keepdims=True
        )
        trace = jnp.sum(trace, axis=1, keepdims=True)
        scale = 1.0 / (jnp.sqrt(trace) + 1e-07)
        dot = lambda a, b: jnp.dot(a[...], b[...], preferred_element_type=F32)

        gram[...] = gram_in[...] * scale * scale
        gram_b[...] = gram[...].astype(BF16)
        for lin, lin_b in ((lin0, lin0_b), (lin1, lin1_b)):
            lin[...] = COEF_B * gram[...] + COEF_C * dot(gram_b, gram_b)
            lin_b[...] = lin[...].astype(BF16)
            term[...] = COEF_A * gram[...] + dot(lin_b, gram_b)
            term_b[...] = term[...].astype(BF16)
            gram[...] = COEF_A * term[...] + dot(lin_b, term_b)
            gram_b[...] = gram[...].astype(BF16)
        lin0[...] = COEF_A * (lin0[...] + lin1[...]) + dot(lin0_b, lin1_b)
        lin0_b[...] = lin0[...].astype(BF16)
        lin1[...] = COEF_B * gram[...] + COEF_C * dot(gram_b, gram_b)
        lin1_b[...] = lin1[...].astype(BF16)
        whole = COEF_A**2 * lin1[...] + COEF_A * lin0[...] + dot(lin0_b, lin1_b)
        whole = whole + jnp.where(row_id == col_id, COEF_A**3, 0.0)
        gram_b[...] = (whole * scale).astype(BF16)

        def one(step, carry):
            index = near_band(bands - 1 - step)
            at = pl.ds(index * band, band)
            done[at, :] = jnp.dot(
                rows[at, :], gram_b[...], preferred_element_type=F32
            ).astype(BF16)
            for y_to in range(y_size):
                here = out_stays(index, y_to)

                @pl.when(y_to != y)
                def _():
                    relay_copy(index, y_to).start()

                @pl.when(jnp.logical_and(y_to == y, jnp.logical_not(here)))
                def _():
                    out_copy(index, y_to).start()

                @pl.when(here)
                def _():
                    pltpu.make_async_copy(
                        block(done, index * y_size + y_to), block(out_ref, own_slot),
                        out_recv.at[own_slot],
                    ).start()

            return carry

        lax.fori_loop(0, bands, one, 0)

    def pass_copy(index):
        return remote(
            block(relay, index), block(out_ref, own_slot),
            pass_send.at[index], out_recv.at[own_slot],
            owned_block, out_place(index, y),
        )

    @pl.when(jnp.logical_not(is_owner))
    def _():
        def one(step, carry):
            index = near_band(bands - 1 - step)
            here = block(relay, index)
            pltpu.make_async_copy(here, here, relay_recv.at[index]).wait()
            stay = out_stays(index, y)

            @pl.when(jnp.logical_not(stay))
            def _():
                pass_copy(index).start()

            @pl.when(stay)
            def _():
                pltpu.make_async_copy(
                    block(relay, index), block(out_ref, own_slot), out_recv.at[own_slot]
                ).start()

            return carry

        for stage in (1, 2, 3):
            hand_in(stage, summed(stage - 1))
        lax.fori_loop(0, bands // 4, one, 0)
        hand_in(4, summed(3))
        lax.fori_loop(bands // 4, bands // 2, one, 0)
        score[last] = summed(4)

        @pl.when(skew == 1)
        def _():
            last_copy().start()

        lax.fori_loop(bands // 2, bands, one, 0)

    @pl.when(is_owner)
    def _():
        last_copy().wait_recv()

    tile = score[last]
    id_col = jnp.zeros((8, 128), jnp.int32)
    weight_row = jnp.zeros((1, 128), F32)
    for g in range(groups):
        id_col = jnp.where(sub == g, ids_ref[g], id_col)
        weight_row = jnp.where(lane[:1] == g, weights_ref[g], weight_row)
    column = lambda k: jnp.sum(jnp.where(lane == k, tile, 0.0), axis=1, keepdims=True)
    aligned, squares, total_sq = column(0), column(1), column(2)
    cosine = aligned / (jnp.sqrt(squares) * jnp.sqrt(total_sq) + 1e-06)
    onehot = jnp.where(id_col == lane, 1.0, 0.0)
    kind_counts = jnp.sum(onehot, axis=0, keepdims=True)
    points = jnp.sum(onehot * cosine, axis=0, keepdims=True) / jnp.maximum(kind_counts, 1.0)
    share = weight_row / jnp.full((1, 128), total_weight, F32)
    raised = share * jnp.exp(ETA * points)
    new_ref[...] = raised / jnp.sum(raised, axis=1, keepdims=True)

    for rel, stage in order:
        sib_copy(rel, stage).wait_send()
    for way in (0, 1):
        for stage in (0, 1):
            far_copy(way, stage).wait_send()
        for quarter in range(4):
            near_copy(way, quarter).wait_send()
    for stage in (0, 1):
        for step in range(1, RING):
            ag_copy(step, stage).wait_send()
    for j in range(mats):

        @pl.when(jnp.logical_not(stays(j)))
        def _():
            in_copy(j).wait_send()

    for step in range(1, y_size):

        @pl.when(jnp.logical_not(to_owner(step)))
        def _():
            red_copy(0, step).wait_send()

    @pl.when(skew == 1)
    def _():
        last_copy().wait_send()

    @pl.when(is_owner)
    def _():
        def one(index, carry):
            for y_to in range(y_size):

                @pl.when(jnp.logical_not(out_stays(index, y_to)))
                def _():
                    out_copy(index, y_to).wait_send()

            return carry

        lax.fori_loop(0, bands, one, 0)

    @pl.when(jnp.logical_not(is_owner))
    def _():
        for stage in range(1, 5):
            for step in range(1, stages[stage][0]):
                red_copy(stage, step).wait_send()

        def one(index, carry):

            @pl.when(jnp.logical_not(out_stays(index, y)))
            def _():
                pass_copy(index).wait_send()

            return carry

        lax.fori_loop(0, bands, one, 0)

    for j in range(mats):
        here = block(out_ref, j)
        pltpu.make_async_copy(here, here, out_recv.at[j]).wait()


def body(gradients, row_counts, domain_ids, domain_weights):
    groups = lax.axis_size("domain")
    shards = lax.axis_size("fsdp")
    matrices, height, width = gradients.shape[1:]
    mats = matrices // groups
    y_size = 4 if shards == 64 else 2
    z_size = shards // y_size
    z_low = 4 if z_size == 16 else 2
    sizes = (groups, y_size, z_size, z_low, mats, height, width)
    assert groups == CORES * RING
    block = lambda count: pltpu.VMEM((count * height, width), BF16)
    square = lambda dtype: pltpu.VMEM((width, width), dtype)
    dma = lambda *shape: pltpu.SemaphoreType.DMA(shape)
    red = CORES + RING + y_size + z_low + z_size // z_low + 1
    assert z_size == CORES * mats and mats % y_size == 0
    held = shards // CORES
    finished, new_weights = pl.pallas_call(
        functools.partial(kernel, sizes),
        out_shape=(
            jax.ShapeDtypeStruct((mats * height, width), BF16),
            jax.ShapeDtypeStruct((1, 128), F32),
        ),
        in_specs=[pl.BlockSpec(memory_space=pltpu.SMEM)] * 3
        + [pl.BlockSpec(memory_space=pl.ANY)],
        out_specs=(
            pl.BlockSpec(memory_space=pl.ANY),
            pl.BlockSpec(memory_space=pltpu.VMEM),
        ),
        scratch_shapes=[
            block(RING * mats), block(RING * mats), block(mats), block(2 * mats),
            block(mats), block(2 * mats), block(RING * mats), block(held), block(held), block(z_size // CORES),
            *[square(F32)] * 5,
            *[square(BF16)] * 4,
            pltpu.VMEM((red, 8, 128), F32), pltpu.VMEM((8, width), F32),
            dma(4, 2), dma(4, 2), dma(4, 2), dma(4), dma(4), dma(2, 4), dma(2, 4),
            dma(4, 2), dma(4, 2), dma(mats), dma(z_size // CORES),
            dma(held), dma(mats), dma(z_size // CORES), dma(z_size // CORES), dma(red), dma(red), pltpu.SemaphoreType.DMA,
            pltpu.SemaphoreType.DMA, pltpu.SemaphoreType.REGULAR((3,)),
        ],
        compiler_params=pltpu.CompilerParams(
            collective_id=0, has_side_effects=True, vmem_limit_bytes=60 * 2**20
        ),
        cost_estimate=pl.CostEstimate(
            flops=20 * 10**9, bytes_accessed=8 * 2**20, transcendentals=0
        ),
    )(row_counts, domain_ids, domain_weights, gradients.reshape(matrices * height, width))
    full_rows = height * shards
    updates = finished.reshape(mats, height, width).astype(F32) * (
        MUON_SCALE * math.sqrt(full_rows)
    )
    return (updates, new_weights[0, :groups])


def solution(mesh):
    placed = (P("domain", None, "fsdp", None), P(), P(), P())
    return jax.shard_map(
        body,
        mesh=mesh,
        in_specs=placed,
        out_specs=(P("domain", "fsdp", None), P()),
        check_vma=False,
    )
```
